256 devices in a mesh: row: 32 (over z, x), col: 8 (over y, core).
Axes of the slice: x: 4, y: 4, z: 8, core: 2. Of those that a mesh axis runs over, the one named last changes fastest.
Arguments:
- image: bfloat16 [512, 1024, 256], P('row', 'col'), may hold values from -6 to 6
- kernel_one: bfloat16 [3, 3, 256, 256], replicated, may hold values from -0.125 to 0.125
- kernel_two: bfloat16 [3, 3, 256, 512], replicated, may hold values from -0.125 to 0.125
- cotangent: bfloat16 [256, 512, 512], P('row', 'col'), may hold values from -6 to 6
Outputs:
- image_grad: bfloat16 [512, 1024, 256], P('row', 'col')
- update_one: bfloat16 [3, 3, 256, 256], replicated
- update_two: bfloat16 [3, 3, 256, 512], replicated
The draws below stay inside these ranges and needn't reach their ends.
All inputs are finite; a program needn't handle non-finite values.
Results may differ from the reference program's by a relative error of at most 0.006.
Values may be sent and summed in bfloat16 or wider, within the bound.
A program may use at most 128 MiB of HBM per device.

```python
import jax
import jax.numpy as jnp
from jax import lax

CH = 256
CO = 512
HEIGHT = 512
WIDTH = 1024


def block_levels(own_key, shape, cuts, smallest, high):
    loudness, own = 1.0, jax.random.fold_in(own_key, 6)
    for position, blocks in cuts:
        heights = jnp.exp(jax.random.uniform(jax.random.fold_in(own, position), (blocks,), jnp.float32, smallest / len(cuts), high / len(cuts)))
        loudness = loudness * jnp.repeat(heights, shape[position] // blocks).reshape([-1 if axis == position else 1 for axis in range(len(shape))])
    return loudness


def normal_values(stream_key, shape, width, bound, shards=(), held_as=jnp.bfloat16):
    factor_of = block_levels(stream_key, shape, shards, -0.22, 0.18) if shards else 1.0
    values = jax.random.normal(stream_key, shape, jnp.float32) * width * factor_of
    return jnp.minimum(jnp.maximum(values, -bound), bound).astype(held_as)


def setup_inputs(seed: int = 0) -> dict:
    streams_of = jax.random.split(jax.random.key(seed), 5)
    image = normal_values(streams_of[0], (HEIGHT, WIDTH, CH), 1.0, 6.0, ((0, 32), (1, 8)))
    kernel_one = normal_values(streams_of[1], (3, 3, CH, CH), (9 * CH) ** -0.5, 0.125)
    kernel_two = normal_values(streams_of[2], (3, 3, CH, CO), (9 * CH) ** -0.5, 0.125)
    cotangent = normal_values(streams_of[3], (HEIGHT // 2, WIDTH // 2, CO), 1.0, 6.0, ((0, 32), (1, 8)))
    return {"image": image, "kernel_one": kernel_one, "kernel_two": kernel_two, "cotangent": cotangent}


def conv_plain(source, kernel, padding, dilation, layout):
    result = lax.conv_general_dilated(source.astype(jnp.float32)[None], kernel.astype(jnp.float32), (1, 1), padding, lhs_dilation=dilation, dimension_numbers=('NHWC', layout, 'NHWC'), precision=lax.Precision.HIGHEST, preferred_element_type=jnp.float32)
    return result[0]

def reference(image, kernel_one, kernel_two, cotangent):
    pre_act = conv_plain(image, kernel_one, ((1, 1), (1, 1)), (1, 1), 'HWIO')
    activ = jax.nn.silu(pre_act).astype(jnp.bfloat16)
    act_pad = jnp.pad(activ, ((1, 0), (1, 0), (0, 0)))
    cot_float = cotangent.astype(jnp.float32)
    rows_two = []
    for row_off in range(3):
        cols_two = []
        for col_off in range(3):
            patch = act_pad[row_off:row_off + HEIGHT - 1:2, col_off:col_off + WIDTH - 1:2].astype(jnp.float32)
            cols_two.append(jnp.einsum('ijc,ije->ce', patch, cot_float, precision=lax.Precision.HIGHEST))
        rows_two.append(jnp.stack(cols_two))
    grad_two = jnp.stack(rows_two)
    act_full = conv_plain(cotangent, kernel_two[::-1, ::-1], ((2, 2), (2, 2)), (2, 2), 'HWOI')
    act_grad = act_full[1:, 1:]
    sig = jax.nn.sigmoid(pre_act)
    pre_grad = (act_grad * sig * (1.0 + pre_act * (1.0 - sig))).astype(jnp.bfloat16)
    image_pad = jnp.pad(image, ((1, 1), (1, 1), (0, 0))).astype(jnp.float32)
    grad_float = pre_grad.astype(jnp.float32)
    rows_one = []
    for row_off in range(3):
        cols_one = []
        for col_off in range(3):
            patch = image_pad[row_off:row_off + HEIGHT, col_off:col_off + WIDTH]
            cols_one.append(jnp.einsum('ijc,ijd->cd', patch, grad_float, precision=lax.Precision.HIGHEST))
        rows_one.append(jnp.stack(cols_one))
    grad_one = jnp.stack(rows_one)
    image_grad = conv_plain(pre_grad, kernel_one[::-1, ::-1], ((1, 1), (1, 1)), (1, 1), 'HWOI').astype(jnp.bfloat16)
    update_one = (grad_one * lax.rsqrt(jnp.mean(grad_one * grad_one) + 1e-06)).astype(jnp.bfloat16)
    update_two = (grad_two * lax.rsqrt(jnp.mean(grad_two * grad_two) + 1e-06)).astype(jnp.bfloat16)
    return (image_grad, update_one, update_two)
```

```python
import functools

import jax
import jax.numpy as jnp
from jax import lax
from jax.experimental import pallas as pl
from jax.experimental.pallas import tpu as pltpu
from jax.sharding import PartitionSpec as P

MESH = pl.DeviceIdType.MESH
bf16, f32 = jnp.bfloat16, jnp.float32
ROWS, COLS = 32, 8
NX, NY, NZ = 4, 4, 8
JOBS = ((0, 0, 2304, "yx"), (1, 0, 2304, "xy"), (2, 0, 1280, "yx"), (2, 1280, 1024, "xy"))


def dot(a, b):
    return jnp.dot(a, b, preferred_element_type=f32)


def dot_nt(a, b):
    return lax.dot_general(a, b, (((1,), (1,)), ((), ())), preferred_element_type=f32)


def dot_tn(a, b):
    return lax.dot_general(a, b, (((0,), (0,)), ((), ())), preferred_element_type=f32)


def total_of(terms):
    return functools.reduce(lambda u, v: u + v, terms)


def kernel(
    image_hbm, k1_hbm, k2_hbm, cot_hbm,
    image_grad, two, one,
    image, k1, k2, cot, F, X, V, A, D, C, Cs,
    edge32, edges, hrow, hcol, cedge, crow, ccol, pedges, prow, pcol, left, right,
    T2, R2, T1, R1, S, P1, Q1, P2, Zs, Zr, G,
    load_sem,
    img_s, img_r, cot_s, cot_r, pg_s, pg_r, c2_s, c2_r, c1_s, c1_r,
    a1_s, a1_r, a2_s, a2_r, az_s, az_r, gz_s, gz_r, g2_s, g2_r, g1_s, g1_r, gc_s, gc_r,
):
    row, col = lax.axis_index("row"), lax.axis_index("col")
    z, x, y, core = row // NX, row % NX, col // 2, col % 2
    other = 1 - core

    def at_row(d):
        return (row + d + ROWS) % ROWS

    def at_col(d):
        return (col + d + COLS) % COLS

    def at_x(k):
        return (z * NX + (x + k) % NX, col)

    def at_y(k):
        return (row, ((y + k) % NY) * 2 + core)

    def at_z(k):
        return (((z + k) % NZ) * NX + x, col)

    sibling = (row, y * 2 + other)
    around = [(at_row(u), at_col(v)) for u in (-1, 0, 1) for v in (-1, 0, 1) if (u, v) != (0, 0)]
    pending = []

    def send(src, dst, send_sem, recv_sem, to):
        copy = pltpu.make_async_remote_copy(
            src_ref=src, dst_ref=dst, send_sem=send_sem, recv_sem=recv_sem, device_id=to, device_id_type=MESH
        )
        copy.start()
        pending.append(copy)
        return copy

    loads = []
    for n, (src, dst) in enumerate(((image_hbm, image), (cot_hbm, cot), (k1_hbm, k1), (k2_hbm, k2))):
        copy = pltpu.make_async_copy(src, dst, load_sem.at[n])
        copy.start()
        loads.append(copy)

    barrier = pltpu.get_barrier_semaphore()
    greeted = around + [sibling] + [at_y(k) for k in (1, 2, 3)] + [at_x(k) for k in (1, 2, 3)] + [at_z(k) for k in range(1, NZ)]
    for to in greeted:
        pl.semaphore_signal(barrier, inc=1, device_id=to, device_id_type=MESH)

    def spread(slot, values):
        v = values.astype(f32)
        F[slot, 0] = v[:, :128]
        F[slot, 1] = v[:, 128:]

    loads[0].wait()

    @pl.loop(0, 16)
    def _(p):
        spread(p, image[p])

    for p in range(16):
        for h in range(2):
            edge32[0, p : p + 1, 128 * h : 128 * h + 128] = F[p, h, 0:1, :]
            edge32[1, p : p + 1, 128 * h : 128 * h + 128] = F[p, h, 127:128, :]
    edges[...] = edge32[...].astype(bf16)
    loads[1].wait()
    edge2 = [cot[i, 0:16, :].astype(f32)[0:1] for i in range(8)]
    cedge[...] = jnp.concatenate(edge2 + [jnp.zeros((8, 512), f32)], axis=0).astype(bf16)

    pl.semaphore_wait(barrier, len(greeted))

    def send_halos(first, last, ends, rows_to, cols_to, send_sem, recv_sem):
        sent = [
            send(first, rows_to.at[1], send_sem.at[0], recv_sem.at[0], (at_row(-1), col)),
            send(last, rows_to.at[0], send_sem.at[1], recv_sem.at[1], (at_row(1), col)),
        ]
        n = 2
        for side, v in ((1, -1), (0, 1)):
            for place, u in ((0, 1), (1, 0), (2, -1)):
                to = (at_row(u) if u else row, at_col(v))
                sent.append(send(ends.at[1 - side], cols_to.at[side, place], send_sem.at[n], recv_sem.at[n], to))
                n += 1
        return sent

    halo = send_halos(image.at[0], image.at[15], edges, hrow, hcol, img_s, img_r)
    cot_halo = [
        send(cot.at[0], crow, cot_s.at[0], cot_r.at[0], (at_row(-1), col)),
        send(cedge, ccol.at[0], cot_s.at[1], cot_r.at[1], (row, at_col(-1))),
        send(cedge, ccol.at[1], cot_s.at[2], cot_r.at[2], (at_row(-1), at_col(-1))),
    ]

    def sides_of(cols_to):
        for side, ref, none in ((0, left, col == 0), (1, right, col == COLS - 1)):
            above = jnp.where((row == 0) | none, 0.0, cols_to[side, 0].astype(f32)[15:16])
            mid = jnp.where(none, 0.0, cols_to[side, 1].astype(f32))
            below = jnp.where((row == ROWS - 1) | none, 0.0, cols_to[side, 2].astype(f32)[0:1])
            ref[0:1] = above
            ref[1:17] = mid
            ref[17:18] = below

    first_at = lax.broadcasted_iota(jnp.int32, (64, 256), 0) == 0
    last_at = lax.broadcasted_iota(jnp.int32, (64, 256), 0) == 63

    def shifted(ref, r, even, odd, centre):
        before = jnp.where(first_at, left[pl.ds(r, 1)], pltpu.roll(odd, 1, 0)).astype(bf16)
        after = jnp.where(last_at, right[pl.ds(r, 1)], pltpu.roll(even, 63, 0)).astype(bf16)
        e, o = even.astype(bf16), odd.astype(bf16)
        ref[r, 0:64, 0:256] = before
        ref[r, 64:128, 0:256] = e
        if centre:
            ref[r, 0:64, 256:512] = e
            ref[r, 64:128, 256:512] = o
        ref[r, 0:64, 512:768] = o
        ref[r, 64:128, 512:768] = after

    def columns_of(slot, odd):
        return jnp.concatenate([F[slot, h, pl.ds(odd, 64, stride=2), :] for h in (0, 1)], axis=1)

    for copy in halo:
        copy.wait_recv()
    sides_of(hcol)
    spread(16, jnp.where(row == 0, 0.0, hrow[0].astype(f32)))
    spread(17, jnp.where(row == ROWS - 1, 0.0, hrow[1].astype(f32)))

    @pl.loop(0, 16)
    def _(p):
        shifted(X, p + 1, columns_of(p, 0), columns_of(p, 1), True)

    shifted(X, 0, columns_of(16, 0), columns_of(16, 1), True)
    shifted(X, 17, columns_of(17, 0), columns_of(17, 1), True)

    loads[2].wait()

    @pl.loop(0, 4)
    def _(g):
        acc = total_of(
            [dot(X[pl.ds(4 * g + a, 4)].reshape(512, 768), k1[768 * a : 768 * a + 768, :]) for a in range(3)]
        )
        s = jax.nn.sigmoid(acc)
        act = (acc * s).astype(bf16).reshape(4, 128, 256)
        D[pl.ds(4 * g, 4)] = (s * (1.0 + acc * (1.0 - s))).reshape(4, 128, 256)
        for u in range(4):
            for c in range(2):
                A[u % 2, c, 2 * g + u // 2] = act[u, 64 * c : 64 * c + 64]

    for copy in cot_halo:
        copy.wait_recv()
    no_right, no_below = col == COLS - 1, row == ROWS - 1
    end_at = lax.broadcasted_iota(jnp.int32, (64, 512), 0) == 63
    for i in range(9):
        if i < 8:
            here = cot[i].astype(f32)
            beside = ccol[0].astype(f32)[i : i + 1]
        else:
            here = jnp.where(no_below, 0.0, crow[...].astype(f32))
            beside = jnp.where(no_below, 0.0, ccol[1].astype(f32)[0:1])
        beside = jnp.where(no_right, 0.0, beside)
        C[i] = here.astype(bf16)
        Cs[i] = jnp.where(end_at, beside, pltpu.roll(here, 63, 0)).astype(bf16)

    core_two = []
    for a in range(3):
        first = 1 if a == 0 else 0
        for b in range(3):
            lhs = A[(a + 1) % 2, (b + 1) % 2].reshape(512, 256)
            for h in range(2):
                rhs = (Cs if b == 0 else C)[first : first + 8, :, 256 * h : 256 * h + 256].reshape(512, 256)
                T2[h, (3 * a + b) * 256 : (3 * a + b) * 256 + 256, :] = dot_tn(lhs, rhs).astype(bf16)
        span = pl.ds(768 * a, 768)
        core_two.append(send(T2.at[other, span], R2.at[span], c2_s.at[a], c2_r.at[a], sibling))

    loads[3].wait()

    def tap(a, b):
        return k2[(3 * a + b) * 256 : (3 * a + b) * 256 + 256, :]

    @pl.loop(0, 2)
    def _(g):
        for rp in range(2):
            for cp in range(2):
                terms = []
                for a, d in ((1, 0),) if rp == 0 else ((2, 0), (0, 1)):
                    for b, ref in ((1, C),) if cp == 0 else ((2, C), (0, Cs)):
                        terms.append(dot_nt(ref[pl.ds(4 * g + d, 4)].reshape(256, 512), tap(a, b)))
                acc = total_of(terms).reshape(4, 64, 256)
                for u in range(4):
                    p = 2 * (4 * g + u) + rp
                    V[p + 1, 64 * cp : 64 * cp + 64, 256:512] = (acc[u] * D[p, 64 * cp : 64 * cp + 64]).astype(bf16)

    for p in range(16):
        edge32[0, p : p + 1] = V[p + 1, 0:16, 256:512].astype(f32)[0:1]
        edge32[1, p : p + 1] = V[p + 1, 112:128, 256:512].astype(f32)[15:16]
    pedges[...] = edge32[...].astype(bf16)
    pg_halo = send_halos(V.at[1, :, 256:512], V.at[16, :, 256:512], pedges, prow, pcol, pg_s, pg_r)

    def axis_of(name):
        return (y, at_y, NY) if name == "y" else (x, at_x, NX)

    def places(job):
        j, base, rows, order = job
        o1, o2 = (320, 80) if base else (0, 0)
        return j, base, rows // 4, rows // 16, o1, o2, axis_of(order[0]), axis_of(order[1])

    def spans(job):
        j, base, n1, n2, o1, o2, (i1, _, _), (i2, _, _) = places(job)
        return base + n1 * i1, base + n1 * i1 + n2 * i2

    def al(v):
        return pl.multiple_of(v, 16)

    def stage1(n):
        j, base, n1, n2, o1, o2, (i1, to, _), _ = places(JOBS[n])
        return [
            send(
                S.at[j, pl.ds(al(base + n1 * ((i1 + k) % 4)), n1)], P1.at[j, k - 1, pl.ds(o1, n1)],
                a1_s.at[n, k - 1], a1_r.at[n, k - 1], to(k),
            )
            for k in (1, 2, 3)
        ]

    def stage2(n, arrived):
        j, base, n1, n2, o1, o2, (i1, _, _), (i2, to, _) = places(JOBS[n])
        for copy in arrived:
            copy.wait_recv()
        own = S[j, pl.ds(al(base + n1 * i1), n1)].astype(f32)
        Q1[j, o1 : o1 + n1] = total_of([own] + [P1[j, k, o1 : o1 + n1].astype(f32) for k in range(3)]).astype(bf16)
        return [
            send(
                Q1.at[j, pl.ds(al(o1 + n2 * ((i2 + k) % 4)), n2)], P2.at[j, k - 1, pl.ds(o2, n2)],
                a2_s.at[n, k - 1], a2_r.at[n, k - 1], to(k),
            )
            for k in (1, 2, 3)
        ]

    def stage_z(j, numbers, arrived):
        for copy in arrived:
            copy.wait_recv()
        for n in numbers:
            _, base, n1, n2, o1, o2, _, (i2, _, _) = places(JOBS[n])
            own = Q1[j, pl.ds(al(o1 + n2 * i2), n2)].astype(f32)
            summed = total_of([own] + [P2[j, k, o2 : o2 + n2].astype(f32) for k in range(3)]).astype(bf16)
            for u in range(n2 // 16):
                unit = o2 // 16 + u
                block = summed[16 * u : 16 * u + 16]
                if unit < NZ:
                    Zs[j, unit, 0:16] = block
                else:
                    for k in range(NZ):
                        Zs[j, k, 16:32] = block
        Zr[j, z] = Zs[j, z]
        return [send(Zs.at[j, (z + k) % NZ], Zr.at[j, z], az_s.at[j, k - 1], az_r.at[j, k - 1], at_z(k)) for k in range(1, NZ)]

    def unit_at(j, unit):
        if j < 2:
            return spans(JOBS[j])[1] + 16 * unit
        second = unit // 5
        return (1 - second) * (spans(JOBS[2])[1] + 16 * unit) + second * (spans(JOBS[3])[1] + 16 * (unit - 5))

    def gather_z(j, arrived):
        for copy in arrived:
            copy.wait_recv()
        summed = total_of([Zr[j, k].astype(f32) for k in range(NZ)]).astype(bf16)
        mine = pl.ds(al(unit_at(j, z)), 16)
        G[j, core, mine] = summed[0:16]
        G[j, core, pl.ds(al(unit_at(j, NZ)), 16)] = summed[16:32]
        here = G.at[j, core, mine]
        return [send(here, here, gz_s.at[j, k - 1], gz_r.at[j, k - 1], at_z(k)) for k in range(1, NZ)]

    def gather2(n, arrived):
        j, base, n1, n2, o1, o2, _, (i2, to, _) = places(JOBS[n])
        for copy in arrived:
            copy.wait_recv()
        here = G.at[j, core, pl.ds(al(spans(JOBS[n])[1]), n2)]
        return [send(here, here, g2_s.at[n, k - 1], g2_r.at[n, k - 1], to(k)) for k in (1, 2, 3)]

    def to_sibling(n, k):
        j, base, n1, n2, o1, o2, (i1, _, _), _ = places(JOBS[n])
        here = G.at[j, core, pl.ds(al(base + n1 * ((i1 - k + 4) % 4)), n1)]
        return send(here, here, gc_s.at[n, k], gc_r.at[n, k], sibling)

    def gather1(n, arrived):
        j, base, n1, n2, o1, o2, (i1, to, _), _ = places(JOBS[n])
        for copy in arrived:
            copy.wait_recv()
        here = G.at[j, core, pl.ds(al(spans(JOBS[n])[0]), n1)]
        sent = [send(here, here, g1_s.at[n, k - 1], g1_r.at[n, k - 1], to(k)) for k in (1, 2, 3)]
        return sent, [to_sibling(n, 0)]

    def forward(n, arrived):
        sent, across = arrived
        for k in (1, 2, 3):
            sent[k - 1].wait_recv()
            across.append(to_sibling(n, k))
        return across

    for copy in core_two:
        copy.wait_recv()

    @pl.loop(0, 9)
    def _(g):
        span = pl.ds(pl.multiple_of(256 * g, 256), 256)
        both = T2[core, span].astype(f32) + R2[span].astype(f32)
        S[0, span] = both[:, :128].astype(bf16)
        S[1, span] = both[:, 128:].astype(bf16)

    two_1 = [stage1(0), stage1(1)]

    core_one = []
    for a in range(3):
        for b in range(3):
            lhs = X[a : a + 16, :, 256 * b : 256 * b + 256].reshape(2048, 256)
            out = dot_tn(lhs, V[1:17, :, 256:512].reshape(2048, 256)).astype(bf16)
            for h in range(2):
                T1[h, (3 * a + b) * 256 : (3 * a + b) * 256 + 256, :] = out[:, 128 * h : 128 * h + 128]
        span = pl.ds(768 * a, 768)
        core_one.append(send(T1.at[other, span], R1.at[span], c1_s.at[a], c1_r.at[a], sibling))

    for copy in pg_halo:
        copy.wait_recv()
    sides_of(pcol)

    @pl.loop(0, 16)
    def _(p):
        shifted(V, p + 1, V[p + 1, 0:64, 256:512].astype(f32), V[p + 1, 64:128, 256:512].astype(f32), False)

    for place, r, none in ((0, 0, row == 0), (1, 17, row == ROWS - 1)):
        values = jnp.where(none, 0.0, prow[place].astype(f32))
        shifted(V, r, values[0:64], values[64:128], True)

    for copy in core_one:
        copy.wait_recv()

    @pl.loop(0, 9)
    def _(g):
        span = pl.ds(pl.multiple_of(256 * g, 256), 256)
        S[2, span] = (T1[core, span].astype(f32) + R1[span].astype(f32)).astype(bf16)

    one_1 = [stage1(2), stage1(3)]

    def image_rows(g):
        terms = []
        for a in range(3):
            for b in range(3):
                m = 3 * (2 - a) + (2 - b)
                lhs = V[pl.ds(4 * g + a, 4), :, 256 * b : 256 * b + 256].reshape(512, 256)
                terms.append(dot_nt(lhs, k1[256 * m : 256 * m + 256, :]))
        acc = total_of(terms).reshape(4, 128, 256)
        for u in range(4):
            p = 4 * g + u
            for h in range(2):
                F[p, h, pl.ds(0, 64, stride=2), :] = acc[u, 0:64, 128 * h : 128 * h + 128]
                F[p, h, pl.ds(1, 64, stride=2), :] = acc[u, 64:128, 128 * h : 128 * h + 128]
            image_grad[p] = jnp.concatenate([F[p, 0], F[p, 1]], axis=1).astype(bf16)

    pl.loop(0, 2)(image_rows)
    two_2 = [stage2(0, two_1[0]), stage2(1, two_1[1])]
    pl.loop(2, 4)(image_rows)
    two_z = [stage_z(0, (0,), two_2[0]), stage_z(1, (1,), two_2[1])]
    one_2 = [stage2(2, one_1[0]), stage2(3, one_1[1])]
    two_gz = [gather_z(0, two_z[0]), gather_z(1, two_z[1])]
    one_z = stage_z(2, (2, 3), one_2[0] + one_2[1])
    two_g2 = [gather2(0, two_gz[0]), gather2(1, two_gz[1])]
    one_gz = gather_z(2, one_z)
    two_g1 = [gather1(0, two_g2[0]), gather1(1, two_g2[1])]
    one_g2 = [gather2(2, one_gz), gather2(3, [])]
    one_g1 = [gather1(2, one_g2[0]), gather1(3, one_g2[1])]
    two_c = [forward(0, two_g1[0]), forward(1, two_g1[1])]
    one_c = [forward(2, one_g1[0]), forward(3, one_g1[1])]

    def scale_of(buffers, count):
        def add(g, acc):
            span = pl.ds(pl.multiple_of(256 * g, 256), 256)
            for j in buffers:
                for c in range(2):
                    v = G[j, c, span].astype(f32).reshape(32, 8, 128)
                    acc = acc + jnp.sum(v * v, axis=0)
            return acc

        squares = lax.fori_loop(0, 9, add, jnp.zeros((8, 128), f32))
        return lax.rsqrt(jnp.sum(squares) / count + 1e-06)

    for copy in two_c[0] + two_c[1]:
        copy.wait_recv()
    scale_two = scale_of((0, 1), 9.0 * 256 * 512)

    @pl.loop(0, 9)
    def _(g):
        span = pl.ds(pl.multiple_of(256 * g, 256), 256)
        for c in range(2):
            for j in range(2):
                two[span, 256 * c + 128 * j : 256 * c + 128 * j + 128] = (G[j, c, span].astype(f32) * scale_two).astype(bf16)

    for copy in one_c[0] + one_c[1]:
        copy.wait_recv()
    scale_one = scale_of((2,), 9.0 * 256 * 256)

    @pl.loop(0, 9)
    def _(g):
        span = pl.ds(pl.multiple_of(256 * g, 256), 256)
        for c in range(2):
            one[span, 128 * c : 128 * c + 128] = (G[2, c, span].astype(f32) * scale_one).astype(bf16)

    for copy in pending:
        copy.wait_send()


def on_device(image, kernel_one, kernel_two, cotangent):
    vmem = pl.BlockSpec(memory_space=pltpu.VMEM)
    dma = pltpu.SemaphoreType.DMA
    pairs = [(8,), (3,), (8,), (3,), (3,), (4, 3), (4, 3), (3, 7), (3, 7), (4, 3), (4, 3), (4, 4)]
    scratch = [
        ((16, 128, 256), bf16), ((2304, 256), bf16), ((2304, 512), bf16), ((8, 64, 512), bf16),
        ((18, 2, 128, 128), f32), ((18, 128, 768), bf16), ((18, 128, 768), bf16),
        ((2, 2, 8, 64, 256), bf16), ((16, 128, 256), f32), ((9, 64, 512), bf16), ((9, 64, 512), bf16),
        ((2, 16, 256), f32), ((2, 16, 256), bf16), ((2, 128, 256), bf16), ((2, 3, 16, 256), bf16),
        ((16, 512), bf16), ((64, 512), bf16), ((2, 16, 512), bf16),
        ((2, 16, 256), bf16), ((2, 128, 256), bf16), ((2, 3, 16, 256), bf16),
        ((24, 256), f32), ((24, 256), f32),
        ((2, 2304, 256), bf16), ((2304, 256), bf16), ((2, 2304, 128), bf16), ((2304, 128), bf16),
        ((3, 2304, 128), bf16), ((3, 3, 576, 128), bf16), ((3, 576, 128), bf16), ((3, 3, 144, 128), bf16),
        ((3, 8, 32, 128), bf16), ((3, 8, 32, 128), bf16), ((3, 2, 2304, 128), bf16),
    ]
    image_grad, two, one = pl.pallas_call(
        kernel,
        out_shape=(
            jax.ShapeDtypeStruct((16, 128, 256), bf16),
            jax.ShapeDtypeStruct((2304, 512), bf16),
            jax.ShapeDtypeStruct((2304, 256), bf16),
        ),
        in_specs=[pl.BlockSpec(memory_space=pl.ANY)] * 4,
        out_specs=[vmem] * 3,
        scratch_shapes=[pltpu.VMEM(shape, kind) for shape, kind in scratch] + [dma((4,))] + [dma(s) for s in pairs for _ in range(2)],
        compiler_params=pltpu.CompilerParams(collective_id=0, has_side_effects=True, vmem_limit_bytes=60 << 20),
    )(image, kernel_one.reshape(2304, 256), kernel_two.reshape(2304, 512), cotangent)
    return image_grad, one.reshape(kernel_one.shape), two.reshape(kernel_two.shape)


def solution(mesh):
    placed = (P("row", "col", None), P(), P(), P("row", "col", None))
    return jax.shard_map(
        on_device, mesh=mesh, in_specs=placed, out_specs=(P("row", "col", None), P(), P()), check_vma=False
    )
```

```python
import functools

import jax
import jax.numpy as jnp
from jax import lax
from jax.experimental import pallas as pl
from jax.experimental.pallas import tpu as pltpu
from jax.sharding import PartitionSpec as P

MESH = pl.DeviceIdType.MESH
bf16, f32 = jnp.bfloat16, jnp.float32
ROWS, COLS = 32, 8
NX, NY, NZ = 4, 4, 8
JOBS = (
    (0, 0, 1280, "yx"), (1, 0, 1024, "xy"),
    (0, 1280, 1024, "yx"), (1, 1024, 1280, "xy"),
    (2, 0, 1280, "yx"), (2, 1280, 1024, "xy"),
)


def dot(a, b):
    return jnp.dot(a, b, preferred_element_type=f32)


def dot_nt(a, b):
    return lax.dot_general(a, b, (((1,), (1,)), ((), ())), preferred_element_type=f32)


def dot_tn(a, b):
    return lax.dot_general(a, b, (((0,), (0,)), ((), ())), preferred_element_type=f32)


def total_of(terms):
    return functools.reduce(lambda u, v: u + v, terms)


def kernel(
    image_hbm, k1_hbm, k2_hbm, cot_hbm,
    image_grad, G, squares,
    image, k1, k2, cot, F, X, V, A, D, B, C, Cs,
    edge32, edges, hrow, hcol, cedge, crow, ccol, pedges, prow, pcol, left, right, fixes,
    T2, R2, T1, R1, S, P1, Q1, P2, Zs, Zr,
    load_sem,
    img_s, img_r, cot_s, cot_r, pg_s, pg_r, c2_s, c2_r, c1_s, c1_r,
    a1_s, a1_r, a2_s, a2_r, az_s, az_r, gz_s, gz_r, g2_s, g2_r, g1_s, g1_r, gc_s, gc_r,
):
    row, col = lax.axis_index("row"), lax.axis_index("col")
    z, x, y, core = row // NX, row % NX, col // 2, col % 2
    other = 1 - core

    def at_row(d):
        return (row + d + ROWS) % ROWS

    def at_col(d):
        return (col + d + COLS) % COLS

    def at_x(k):
        return (z * NX + (x + k) % NX, col)

    def at_y(k):
        return (row, ((y + k) % NY) * 2 + core)

    def at_z(k):
        return (((z + k) % NZ) * NX + x, col)

    sibling = (row, y * 2 + other)
    around = [(at_row(u), at_col(v)) for u in (-1, 0, 1) for v in (-1, 0, 1) if (u, v) != (0, 0)]
    pending = []

    def send(src, dst, send_sem, recv_sem, to):
        copy = pltpu.make_async_remote_copy(
            src_ref=src, dst_ref=dst, send_sem=send_sem, recv_sem=recv_sem, device_id=to, device_id_type=MESH
        )
        copy.start()
        pending.append(copy)
        return copy

    loads = []
    for n, (src, dst) in enumerate(((image_hbm, image), (cot_hbm, cot), (k1_hbm, k1), (k2_hbm, k2))):
        copy = pltpu.make_async_copy(src, dst, load_sem.at[n])
        copy.start()
        loads.append(copy)

    barrier = pltpu.get_barrier_semaphore()
    greeted = around + [sibling] + [at_y(k) for k in (1, 2, 3)] + [at_x(k) for k in (1, 2, 3)] + [at_z(k) for k in range(1, NZ)]
    for to in greeted:
        pl.semaphore_signal(barrier, inc=1, device_id=to, device_id_type=MESH)

    def spread(slot, values):
        v = values.astype(f32)
        F[slot, 0] = v[:, :128]
        F[slot, 1] = v[:, 128:]

    loads[0].wait()

    @pl.loop(0, 16)
    def _(p):
        spread(p, image[p])

    for p in range(16):
        for h in range(2):
            edge32[0, p : p + 1, 128 * h : 128 * h + 128] = F[p, h, 0:1, :]
            edge32[1, p : p + 1, 128 * h : 128 * h + 128] = F[p, h, 127:128, :]
    edges[...] = edge32[...].astype(bf16)

    first_at = lax.broadcasted_iota(jnp.int32, (64, 256), 0) == 0
    last_at = lax.broadcasted_iota(jnp.int32, (64, 256), 0) == 63

    def shifted(ref, r, even, odd, before_first, after_last, centre):
        before = jnp.where(first_at, before_first, pltpu.roll(odd, 1, 0)).astype(bf16)
        after = jnp.where(last_at, after_last, pltpu.roll(even, 63, 0)).astype(bf16)
        e, o = even.astype(bf16), odd.astype(bf16)
        ref[r, 0:64, 0:256] = before
        ref[r, 64:128, 0:256] = e
        if centre:
            ref[r, 0:64, 256:512] = e
            ref[r, 64:128, 256:512] = o
        ref[r, 0:64, 512:768] = o
        ref[r, 64:128, 512:768] = after

    def columns_of(slot, odd):
        return jnp.concatenate([F[slot, h, pl.ds(odd, 64, stride=2), :] for h in (0, 1)], axis=1)

    @pl.loop(0, 16)
    def _(p):
        shifted(X, p + 1, columns_of(p, 0), columns_of(p, 1), 0.0, 0.0, True)

    X[0] = jnp.zeros((128, 768), bf16)
    X[17] = jnp.zeros((128, 768), bf16)

    loads[1].wait()
    edge2 = [cot[i, 0:16, :].astype(f32)[0:1] for i in range(8)]
    cedge[...] = jnp.concatenate(edge2 + [jnp.zeros((8, 512), f32)], axis=0).astype(bf16)
    pl.semaphore_wait(barrier, len(greeted))

    def send_halos(first, last, ends, rows_to, cols_to, send_sem, recv_sem):
        sent = [
            send(first, rows_to.at[1], send_sem.at[0], recv_sem.at[0], (at_row(-1), col)),
            send(last, rows_to.at[0], send_sem.at[1], recv_sem.at[1], (at_row(1), col)),
        ]
        n = 2
        for side, v in ((1, -1), (0, 1)):
            for place, u in ((0, 1), (1, 0), (2, -1)):
                to = (at_row(u) if u else row, at_col(v))
                sent.append(send(ends.at[1 - side], cols_to.at[side, place], send_sem.at[n], recv_sem.at[n], to))
                n += 1
        return sent

    halo = send_halos(image.at[0], image.at[15], edges, hrow, hcol, img_s, img_r)
    cot_halo = [
        send(cot.at[0], crow, cot_s.at[0], cot_r.at[0], (at_row(-1), col)),
        send(cedge, ccol.at[0], cot_s.at[1], cot_r.at[1], (row, at_col(-1))),
        send(cedge, ccol.at[1], cot_s.at[2], cot_r.at[2], (at_row(-1), at_col(-1))),
    ]

    end_at = lax.broadcasted_iota(jnp.int32, (64, 512), 0) == 63
    for i in range(8):
        C[i] = cot[i]
        Cs[i] = jnp.where(end_at, 0.0, pltpu.roll(cot[i].astype(f32), 63, 0)).astype(bf16)
    C[8] = jnp.zeros((64, 512), bf16)
    Cs[8] = jnp.zeros((64, 512), bf16)

    loads[2].wait()

    @pl.loop(0, 4)
    def _(g):
        acc = total_of(
            [dot(X[pl.ds(4 * g + a, 4)].reshape(512, 768), k1[768 * a : 768 * a + 768, :]) for a in range(3)]
        )
        D[pl.ds(4 * g, 4)] = acc.reshape(4, 128, 256)

    loads[3].wait()

    def tap(a, b):
        return k2[(3 * a + b) * 256 : (3 * a + b) * 256 + 256, :]

    @pl.loop(0, 2)
    def _(g):
        for rp in range(2):
            for cp in range(2):
                terms = []
                for a, d in ((1, 0),) if rp == 0 else ((2, 0), (0, 1)):
                    for b, ref in ((1, C),) if cp == 0 else ((2, C), (0, Cs)):
                        terms.append(dot_nt(ref[pl.ds(4 * g + d, 4)].reshape(256, 512), tap(a, b)))
                acc = total_of(terms).reshape(4, 64, 256)
                for u in range(4):
                    B[2 * (4 * g + u) + rp, 64 * cp : 64 * cp + 64] = acc[u]

    def sides_of(cols_to):
        for side, ref, none in ((0, left, col == 0), (1, right, col == COLS - 1)):
            above = jnp.where((row == 0) | none, 0.0, cols_to[side, 0].astype(f32)[15:16])
            mid = jnp.where(none, 0.0, cols_to[side, 1].astype(f32))
            below = jnp.where((row == ROWS - 1) | none, 0.0, cols_to[side, 2].astype(f32)[0:1])
            ref[0:1] = above
            ref[1:17] = mid
            ref[17:18] = below

    for copy in halo:
        copy.wait_recv()
    sides_of(hcol)
    spread(16, jnp.where(row == 0, 0.0, hrow[0].astype(f32)))
    spread(17, jnp.where(row == ROWS - 1, 0.0, hrow[1].astype(f32)))
    for slot, r in ((16, 0), (17, 17)):
        shifted(X, r, columns_of(slot, 0), columns_of(slot, 1), left[r : r + 1], right[r : r + 1], True)
    top_at = lax.broadcasted_iota(jnp.int32, (16, 256), 0) == 0
    low_at = lax.broadcasted_iota(jnp.int32, (16, 256), 0) == 15
    for r in range(1, 17):
        X[r, 0:16, 0:256] = jnp.where(top_at, left[r : r + 1], X[r, 0:16, 0:256].astype(f32)).astype(bf16)
        X[r, 112:128, 512:768] = jnp.where(low_at, right[r : r + 1], X[r, 112:128, 512:768].astype(f32)).astype(bf16)
    D[0] += dot(X[0], k1[0:768, :])
    D[15] += dot(X[17], k1[1536:2304, :])
    for side, ref, b in ((0, left, 0), (1, right, 2)):
        ref[0:1] = jnp.zeros((1, 256), f32)
        ref[17:18] = jnp.zeros((1, 256), f32)
        fixes[side] = total_of(
            [dot(ref[a : a + 16].astype(bf16), k1[(3 * a + b) * 256 : (3 * a + b) * 256 + 256, :]) for a in range(3)]
        )
        at = 127 * side
        for p in range(16):
            D[p, at : at + 1] += fixes[side, p : p + 1]

    for copy in cot_halo:
        copy.wait_recv()
    no_right, no_below = col == COLS - 1, row == ROWS - 1
    beside = jnp.where(no_right, 0.0, ccol[0].astype(f32))
    corner = jnp.where(no_right | no_below, 0.0, ccol[1].astype(f32)[0:1])
    under = jnp.where(no_below, 0.0, crow[...].astype(f32))
    C[8] = under.astype(bf16)
    Cs[8] = jnp.where(end_at, corner, pltpu.roll(under, 63, 0)).astype(bf16)
    foot_at = lax.broadcasted_iota(jnp.int32, (16, 512), 0) == 15
    for i in range(8):
        Cs[i, 48:64] = jnp.where(foot_at, beside[i : i + 1], Cs[i, 48:64].astype(f32)).astype(bf16)
    B[15, 0:64] += dot_nt(C[8], tap(0, 1))
    B[15, 64:128] += dot_nt(C[8], tap(0, 2)) + dot_nt(Cs[8], tap(0, 0))
    for a in range(3):
        fixes[a] = dot_nt(beside.astype(bf16), tap(a, 0))
    for i in range(8):
        B[2 * i, 127:128] += fixes[1, i : i + 1]
        below = fixes[2, i : i + 1]
        B[2 * i + 1, 127:128] += below + fixes[0, i + 1 : i + 2] if i < 7 else below

    @pl.loop(0, 8)
    def _(i):
        for rp in range(2):
            pre = D[2 * i + rp]
            s = jax.nn.sigmoid(pre)
            act = (pre * s).astype(bf16)
            for c in range(2):
                A[rp, c, i] = act[64 * c : 64 * c + 64]
            V[2 * i + rp + 1, :, 256:512] = (B[2 * i + rp] * s * (1.0 + pre * (1.0 - s))).astype(bf16)

    for p in range(16):
        edge32[0, p : p + 1] = V[p + 1, 0:16, 256:512].astype(f32)[0:1]
        edge32[1, p : p + 1] = V[p + 1, 112:128, 256:512].astype(f32)[15:16]
    pedges[...] = edge32[...].astype(bf16)
    pg_halo = send_halos(V.at[1, :, 256:512], V.at[16, :, 256:512], pedges, prow, pcol, pg_s, pg_r)

    def axis_of(name):
        return (y, at_y, NY) if name == "y" else (x, at_x, NX)

    def places(job):
        j, base, rows, order = job
        place = JOBS.index(job)
        first = JOBS[place - 1][2] if place % 2 else 0
        o1, o2 = first // 4, first // 16
        return j, base, rows // 4, rows // 16, o1, o2, axis_of(order[0]), axis_of(order[1])

    def spans(job):
        j, base, n1, n2, o1, o2, (i1, _, _), (i2, _, _) = places(job)
        return base + n1 * i1, base + n1 * i1 + n2 * i2

    def al(v):
        return pl.multiple_of(v, 16)

    def stage1(n):
        j, base, n1, n2, o1, o2, (i1, to, _), _ = places(JOBS[n])
        return [
            send(
                S.at[j, pl.ds(al(base + n1 * ((i1 + k) % 4)), n1)], P1.at[n // 2, k - 1, pl.ds(o1, n1)],
                a1_s.at[n, k - 1], a1_r.at[n, k - 1], to(k),
            )
            for k in (1, 2, 3)
        ]

    def stage2(n, arrived):
        j, base, n1, n2, o1, o2, (i1, _, _), (i2, to, _) = places(JOBS[n])
        for copy in arrived:
            copy.wait_recv()
        own = S[j, pl.ds(al(base + n1 * i1), n1)].astype(f32)
        Q1[n // 2, o1 : o1 + n1] = total_of([own] + [P1[n // 2, k, o1 : o1 + n1].astype(f32) for k in range(3)]).astype(bf16)
        return [
            send(
                Q1.at[n // 2, pl.ds(al(o1 + n2 * ((i2 + k) % 4)), n2)], P2.at[n // 2, k - 1, pl.ds(o2, n2)],
                a2_s.at[n, k - 1], a2_r.at[n, k - 1], to(k),
            )
            for k in (1, 2, 3)
        ]

    def stage_z(j, arrived):
        for copy in arrived:
            copy.wait_recv()
        for n in (2 * j, 2 * j + 1):
            _, base, n1, n2, o1, o2, _, (i2, _, _) = places(JOBS[n])
            own = Q1[j, pl.ds(al(o1 + n2 * i2), n2)].astype(f32)
            summed = total_of([own] + [P2[j, k, o2 : o2 + n2].astype(f32) for k in range(3)]).astype(bf16)
            for u in range(n2 // 16):
                unit = o2 // 16 + u
                block = summed[16 * u : 16 * u + 16]
                if unit < NZ:
                    Zs[j, unit, 0:16] = block
                else:
                    for k in range(NZ):
                        Zs[j, k, 16:32] = block
        Zr[j, z] = Zs[j, z]
        return [send(Zs.at[j, (z + k) % NZ], Zr.at[j, z], az_s.at[j, k - 1], az_r.at[j, k - 1], at_z(k)) for k in range(1, NZ)]

    def unit_at(g, unit):
        units = JOBS[2 * g][2] // 256
        return spans(JOBS[2 * g])[1] + 16 * unit, spans(JOBS[2 * g + 1])[1] + 16 * (unit - units), (unit + 8 - units) // 8

    def gather_z(g, arrived):
        for copy in arrived:
            copy.wait_recv()
        summed = total_of([Zr[g, k].astype(f32) for k in range(NZ)]).astype(bf16)
        in_first, in_second, second = unit_at(g, z)
        j0, j1 = JOBS[2 * g][0], JOBS[2 * g + 1][0]
        j = j0 + second * (j1 - j0)
        mine = pl.ds(al((1 - second) * in_first + second * in_second), 16)
        G[j, core, mine] = summed[0:16]
        G[j1, core, pl.ds(al(unit_at(g, NZ)[1]), 16)] = summed[16:32]
        here = G.at[j, core, mine]
        return [send(here, here, gz_s.at[g, k - 1], gz_r.at[g, k - 1], at_z(k)) for k in range(1, NZ)]

    def gather2(n, arrived):
        j, base, n1, n2, o1, o2, _, (i2, to, _) = places(JOBS[n])
        for copy in arrived:
            copy.wait_recv()
        here = G.at[j, core, pl.ds(al(spans(JOBS[n])[1]), n2)]
        return [send(here, here, g2_s.at[n, k - 1], g2_r.at[n, k - 1], to(k)) for k in (1, 2, 3)]

    def to_sibling(n, k):
        j, base, n1, n2, o1, o2, (i1, _, _), _ = places(JOBS[n])
        here = G.at[j, core, pl.ds(al(base + n1 * ((i1 - k + 4) % 4)), n1)]
        return send(here, here, gc_s.at[n, k], gc_r.at[n, k], sibling)

    def gather1(n, arrived):
        j, base, n1, n2, o1, o2, (i1, to, _), _ = places(JOBS[n])
        for copy in arrived:
            copy.wait_recv()
        here = G.at[j, core, pl.ds(al(spans(JOBS[n])[0]), n1)]
        sent = [send(here, here, g1_s.at[n, k - 1], g1_r.at[n, k - 1], to(k)) for k in (1, 2, 3)]
        return sent, [to_sibling(n, 0)]

    def forward(n, arrived):
        sent, across = arrived
        for k in (1, 2, 3):
            sent[k - 1].wait_recv()
            across.append(to_sibling(n, k))
        return across

    def two_taps(first_tap, last_tap, n):
        for m in range(first_tap, last_tap):
            a, b = m // 3, m % 3
            first = 1 if a == 0 else 0
            lhs = A[(a + 1) % 2, (b + 1) % 2].reshape(512, 256)
            rhs = (Cs if b == 0 else C)[first : first + 8].reshape(512, 512)
            out = dot_tn(lhs, rhs).astype(bf16)
            for h in range(2):
                T2[h, 256 * m : 256 * m + 256, :] = out[:, 256 * h : 256 * h + 256]
        span = pl.ds(256 * first_tap, 256 * (last_tap - first_tap))
        return send(T2.at[other, span], R2.at[span], c2_s.at[n], c2_r.at[n], sibling)

    def both_two(copies, first_tap, last_tap):
        for copy in copies:
            copy.wait_recv()

        @pl.loop(first_tap, last_tap)
        def _(g):
            span = pl.ds(pl.multiple_of(256 * g, 256), 256)
            both = T2[core, span].astype(f32) + R2[span].astype(f32)
            S[0, span] = both[:, :128].astype(bf16)
            S[1, span] = both[:, 128:].astype(bf16)

    def one_taps(a):
        for b in range(3):
            lhs = X[a : a + 16, :, 256 * b : 256 * b + 256].reshape(2048, 256)
            out = dot_tn(lhs, V[1:17, :, 256:512].reshape(2048, 256)).astype(bf16)
            for h in range(2):
                T1[h, (3 * a + b) * 256 : (3 * a + b) * 256 + 256, :] = out[:, 128 * h : 128 * h + 128]
        span = pl.ds(768 * a, 768)
        return send(T1.at[other, span], R1.at[span], c1_s.at[a], c1_r.at[a], sibling)

    core_two = [two_taps(0, 3, 0), two_taps(3, 5, 1), two_taps(5, 7, 2), two_taps(7, 9, 3)]
    both_two(core_two[:2], 0, 5)
    g0 = [stage1(0), stage1(1)]
    core_one = [one_taps(0)]
    both_two(core_two[2:], 5, 9)
    g1 = [stage1(2), stage1(3)]
    core_one += [one_taps(1), one_taps(2)]

    for copy in pg_halo:
        copy.wait_recv()
    sides_of(pcol)

    @pl.loop(0, 16)
    def _(p):
        shifted(
            V, p + 1, V[p + 1, 0:64, 256:512].astype(f32), V[p + 1, 64:128, 256:512].astype(f32),
            left[pl.ds(p + 1, 1)], right[pl.ds(p + 1, 1)], False,
        )

    for place, r, none in ((0, 0, row == 0), (1, 17, row == ROWS - 1)):
        values = jnp.where(none, 0.0, prow[place].astype(f32))
        shifted(V, r, values[0:64], values[64:128], left[r : r + 1], right[r : r + 1], True)

    for copy in core_one:
        copy.wait_recv()

    @pl.loop(0, 9)
    def _(g):
        span = pl.ds(pl.multiple_of(256 * g, 256), 256)
        S[2, span] = (T1[core, span].astype(f32) + R1[span].astype(f32)).astype(bf16)

    g2 = [stage1(4), stage1(5)]

    def image_rows(g):
        terms = []
        for a in range(3):
            for b in range(3):
                m = 3 * (2 - a) + (2 - b)
                lhs = V[pl.ds(4 * g + a, 4), :, 256 * b : 256 * b + 256].reshape(512, 256)
                terms.append(dot_nt(lhs, k1[256 * m : 256 * m + 256, :]))
        acc = total_of(terms).reshape(4, 128, 256)
        for u in range(4):
            p = 4 * g + u
            for h in range(2):
                F[p, h, pl.ds(0, 64, stride=2), :] = acc[u, 0:64, 128 * h : 128 * h + 128]
                F[p, h, pl.ds(1, 64, stride=2), :] = acc[u, 64:128, 128 * h : 128 * h + 128]
            image_grad[p] = jnp.concatenate([F[p, 0], F[p, 1]], axis=1).astype(bf16)

    pl.loop(0, 4)(image_rows)

    def pair(step, g, arrived):
        return [step(2 * g, arrived[0]), step(2 * g + 1, arrived[1])]

    def both(arrived):
        return arrived[0] + arrived[1]

    def arrive(across):
        for copy in both(across):
            copy.wait_recv()

    g0 = pair(stage2, 0, g0)
    g1 = pair(stage2, 1, g1)
    g0 = stage_z(0, both(g0))
    g2 = pair(stage2, 2, g2)
    g1 = stage_z(1, both(g1))
    g0 = gather_z(0, g0)
    g2 = stage_z(2, both(g2))
    g1 = gather_z(1, g1)
    g0 = pair(gather2, 0, [g0, []])
    g2 = gather_z(2, g2)
    g1 = pair(gather2, 1, [g1, []])
    g0 = pair(gather1, 0, g0)
    g2 = pair(gather2, 2, [g2, []])
    g1 = pair(gather1, 1, g1)
    g2 = pair(gather1, 2, g2)
    g0 = pair(forward, 0, g0)
    g1 = pair(forward, 1, g1)

    def squares_of(buffers):
        def add(g, acc):
            span = pl.ds(pl.multiple_of(256 * g, 256), 256)
            for j in buffers:
                for c in range(2):
                    v = G[j, c, span].astype(f32).reshape(32, 8, 128)
                    acc = acc + jnp.sum(v * v, axis=0)
            return acc

        return lax.fori_loop(0, 9, add, jnp.zeros((8, 128), f32))

    arrive(g0)
    arrive(g1)
    squares[0] = squares_of((0, 1))
    g2 = pair(forward, 2, g2)
    arrive(g2)
    squares[1] = squares_of((2,))

    for copy in pending:
        copy.wait_send()


def scaled(rows, G, squares, image_grad, two, one, two_v, one_v, sem):
    copies = [pltpu.make_async_copy(rows, image_grad, sem.at[0])]
    copies[0].start()
    scale = [lax.rsqrt(jnp.sum(squares[n]) / count + 1e-06) for n, count in ((0, 9.0 * 256 * 512), (1, 9.0 * 256 * 256))]
    for a in range(3):
        span = pl.ds(768 * a, 768)
        for c in range(2):
            for j in range(2):
                two_v[span, 256 * c + 128 * j : 256 * c + 128 * j + 128] = (G[j, c, span].astype(f32) * scale[0]).astype(bf16)
            one_v[span, 128 * c : 128 * c + 128] = (G[2, c, span].astype(f32) * scale[1]).astype(bf16)
        for n, (src, dst) in enumerate(((two_v, two), (one_v, one))):
            copies.append(pltpu.make_async_copy(src.at[span], dst.at[span], sem.at[1 + 2 * a + n]))
            copies[-1].start()
    for copy in copies:
        copy.wait()


def on_device(image, kernel_one, kernel_two, cotangent):
    vmem = pl.BlockSpec(memory_space=pltpu.VMEM)
    hbm = pl.BlockSpec(memory_space=pl.ANY)
    dma = pltpu.SemaphoreType.DMA
    pairs = [(8,), (3,), (8,), (4,), (3,), (6, 3), (6, 3), (3, 7), (3, 7), (6, 3), (6, 3), (6, 4)]
    scratch = [
        ((16, 128, 256), bf16), ((2304, 256), bf16), ((2304, 512), bf16), ((8, 64, 512), bf16),
        ((18, 2, 128, 128), f32), ((18, 128, 768), bf16), ((18, 128, 768), bf16),
        ((2, 2, 8, 64, 256), bf16), ((16, 128, 256), f32), ((16, 128, 256), f32), ((9, 64, 512), bf16), ((9, 64, 512), bf16),
        ((2, 16, 256), f32), ((2, 16, 256), bf16), ((2, 128, 256), bf16), ((2, 3, 16, 256), bf16),
        ((16, 512), bf16), ((64, 512), bf16), ((2, 16, 512), bf16),
        ((2, 16, 256), bf16), ((2, 128, 256), bf16), ((2, 3, 16, 256), bf16),
        ((24, 256), f32), ((24, 256), f32), ((3, 16, 256), f32),
        ((2, 2304, 256), bf16), ((2304, 256), bf16), ((2, 2304, 128), bf16), ((2304, 128), bf16),
        ((3, 2304, 128), bf16), ((3, 3, 576, 128), bf16), ((3, 576, 128), bf16), ((3, 3, 144, 128), bf16),
        ((3, 8, 32, 128), bf16), ((3, 8, 32, 128), bf16),
    ]
    kept = [pltpu.VMEM((16, 128, 256), bf16), pltpu.VMEM((3, 2, 2304, 128), bf16), pltpu.VMEM((2, 8, 128), f32)]
    rows, sums, squares = pl.pallas_call(
        kernel,
        out_shape=kept,
        in_specs=[hbm] * 4,
        out_specs=[vmem] * 3,
        scratch_shapes=[pltpu.VMEM(shape, kind) for shape, kind in scratch] + [dma((4,))] + [dma(s) for s in pairs for _ in range(2)],
        compiler_params=pltpu.CompilerParams(collective_id=0, has_side_effects=True, vmem_limit_bytes=50 << 20),
    )(image, kernel_one.reshape(2304, 256), kernel_two.reshape(2304, 512), cotangent)
    image_grad, two, one = pl.pallas_call(
        scaled,
        out_shape=(
            jax.ShapeDtypeStruct((16, 128, 256), bf16),
            jax.ShapeDtypeStruct((2304, 512), bf16),
            jax.ShapeDtypeStruct((2304, 256), bf16),
        ),
        in_specs=[vmem] * 3,
        out_specs=[hbm] * 3,
        scratch_shapes=[pltpu.VMEM((2304, 512), bf16), pltpu.VMEM((2304, 256), bf16), dma((7,))],
        compiler_params=pltpu.CompilerParams(vmem_limit_bytes=16 << 20),
    )(rows, sums, squares)
    return image_grad, one.reshape(kernel_one.shape), two.reshape(kernel_two.shape)


def solution(mesh):
    placed = (P("row", "col", None), P(), P(), P("row", "col", None))
    return jax.shard_map(
        on_device, mesh=mesh, in_specs=placed, out_specs=(P("row", "col", None), P(), P()), check_vma=False
    )
```

```python
import functools

import jax
import jax.numpy as jnp
from jax import lax
from jax.experimental import pallas as pl
from jax.experimental.pallas import tpu as pltpu
from jax.sharding import PartitionSpec as P

MESH = pl.DeviceIdType.MESH
bf16, f32 = jnp.bfloat16, jnp.float32
ROWS, COLS = 32, 8
NX, NY, NZ = 4, 4, 8
NEAR, ALONG_Z = (2, 1, 3), (4, 3, 5, 2, 6, 1, 7)
JOBS = (
    (0, 0, 1280, "yx"), (1, 0, 1024, "xy"),
    (0, 1280, 1024, "yx"), (1, 1024, 1280, "xy"),
    (2, 0, 768, "yx"), (2, 768, 512, "xy"),
    (2, 1280, 512, "yx"), (2, 1792, 512, "xy"),
)


def dot(a, b):
    return jnp.dot(a, b, preferred_element_type=f32)


def dot_nt(a, b):
    return lax.dot_general(a, b, (((1,), (1,)), ((), ())), preferred_element_type=f32)


def dot_tn(a, b):
    return lax.dot_general(a, b, (((0,), (0,)), ((), ())), preferred_element_type=f32)


def total_of(terms):
    return functools.reduce(lambda u, v: u + v, terms)


def kernel(
    image_hbm, k1_hbm, k2_hbm, cot_hbm,
    image_grad, two, G, squares,
    image, k1, k2, cot, F, X, V, A, D, B, C, Cs,
    edge32, edges, hrow, hcol, cedge, crow, ccol, pedges, plast, prow, pcol, left, right, fixes,
    T2, R2, T1, R1, S, P1, Q1, P2, Zs, Zr,
    load_sem,
    img_s, img_r, cot_s, cot_r, pg_s, pg_r, c2_s, c2_r, c1_s, c1_r,
    a1_s, a1_r, a2_s, a2_r, az_s, az_r, gz_s, gz_r, g2_s, g2_r, g1_s, g1_r, gc_s, gc_r,
):
    row, col = lax.axis_index("row"), lax.axis_index("col")
    z, x, y, core = row // NX, row % NX, col // 2, col % 2
    other = 1 - core

    def at_row(d):
        return (row + d + ROWS) % ROWS

    def at_col(d):
        return (col + d + COLS) % COLS

    def at_x(k):
        return (z * NX + (x + k) % NX, col)

    def at_y(k):
        return (row, ((y + k) % NY) * 2 + core)

    def at_z(k):
        return (((z + k) % NZ) * NX + x, col)

    sibling = (row, y * 2 + other)
    around = [(at_row(u), at_col(v)) for u in (-1, 0, 1) for v in (-1, 0, 1) if (u, v) != (0, 0)]
    pending = []

    def send(src, dst, send_sem, recv_sem, to):
        copy = pltpu.make_async_remote_copy(
            src_ref=src, dst_ref=dst, send_sem=send_sem, recv_sem=recv_sem, device_id=to, device_id_type=MESH
        )
        copy.start()
        pending.append(copy)
        return copy

    loads = []
    for n, (src, dst) in enumerate(((image_hbm, image), (cot_hbm, cot), (k1_hbm, k1), (k2_hbm, k2))):
        copy = pltpu.make_async_copy(src, dst, load_sem.at[n])
        copy.start()
        loads.append(copy)

    barrier = pltpu.get_barrier_semaphore()
    greeted = around + [sibling] + [at_y(k) for k in (1, 2, 3)] + [at_x(k) for k in (1, 2, 3)] + [at_z(k) for k in range(1, NZ)]
    for to in greeted:
        pl.semaphore_signal(barrier, inc=1, device_id=to, device_id_type=MESH)

    def spread(slot, values):
        v = values.astype(f32)
        F[slot, 0] = v[:, :128]
        F[slot, 1] = v[:, 128:]

    loads[0].wait()

    @pl.loop(0, 16)
    def _(p):
        spread(p, image[p])

    for p in range(16):
        for h in range(2):
            edge32[0, p : p + 1, 128 * h : 128 * h + 128] = F[p, h, 0:1, :]
            edge32[1, p : p + 1, 128 * h : 128 * h + 128] = F[p, h, 127:128, :]
    edges[...] = edge32[...].astype(bf16)

    first_at = lax.broadcasted_iota(jnp.int32, (64, 256), 0) == 0
    last_at = lax.broadcasted_iota(jnp.int32, (64, 256), 0) == 63

    def shifted(ref, r, even, odd, before_first, after_last, centre):
        before = jnp.where(first_at, before_first, pltpu.roll(odd, 1, 0)).astype(bf16)
        after = jnp.where(last_at, after_last, pltpu.roll(even, 63, 0)).astype(bf16)
        e, o = even.astype(bf16), odd.astype(bf16)
        ref[r, 0:64, 0:256] = before
        ref[r, 64:128, 0:256] = e
        if centre:
            ref[r, 0:64, 256:512] = e
            ref[r, 64:128, 256:512] = o
        ref[r, 0:64, 512:768] = o
        ref[r, 64:128, 512:768] = after

    def columns_of(slot, odd):
        return jnp.concatenate([F[slot, h, pl.ds(odd, 64, stride=2), :] for h in (0, 1)], axis=1)

    @pl.loop(0, 16)
    def _(p):
        shifted(X, p + 1, columns_of(p, 0), columns_of(p, 1), 0.0, 0.0, True)

    X[0] = jnp.zeros((128, 768), bf16)
    X[17] = jnp.zeros((128, 768), bf16)

    loads[1].wait()
    edge2 = [cot[i, 0:16, :].astype(f32)[0:1] for i in range(8)]
    cedge[...] = jnp.concatenate(edge2 + [jnp.zeros((8, 512), f32)], axis=0).astype(bf16)
    pl.semaphore_wait(barrier, len(greeted))

    def send_halos(first, last, ends, rows_to, cols_to, send_sem, recv_sem):
        sent = [
            send(first, rows_to.at[1], send_sem.at[0], recv_sem.at[0], (at_row(-1), col)),
            send(last, rows_to.at[0], send_sem.at[1], recv_sem.at[1], (at_row(1), col)),
        ]
        n = 2
        for side, v in ((1, -1), (0, 1)):
            for place, u in ((0, 1), (1, 0), (2, -1)):
                to = (at_row(u) if u else row, at_col(v))
                sent.append(send(ends.at[1 - side], cols_to.at[side, place], send_sem.at[n], recv_sem.at[n], to))
                n += 1
        return sent

    halo = send_halos(image.at[0], image.at[15], edges, hrow, hcol, img_s, img_r)
    cot_halo = [
        send(cot.at[0], crow, cot_s.at[0], cot_r.at[0], (at_row(-1), col)),
        send(cedge, ccol.at[0], cot_s.at[1], cot_r.at[1], (row, at_col(-1))),
        send(cedge, ccol.at[1], cot_s.at[2], cot_r.at[2], (at_row(-1), at_col(-1))),
    ]

    end_at = lax.broadcasted_iota(jnp.int32, (64, 512), 0) == 63
    for i in range(8):
        C[i] = cot[i]
        Cs[i] = jnp.where(end_at, 0.0, pltpu.roll(cot[i].astype(f32), 63, 0)).astype(bf16)
    C[8] = jnp.zeros((64, 512), bf16)
    Cs[8] = jnp.zeros((64, 512), bf16)

    loads[2].wait()

    @pl.loop(0, 4)
    def _(g):
        acc = total_of(
            [dot(X[pl.ds(4 * g + a, 4)].reshape(512, 768), k1[768 * a : 768 * a + 768, :]) for a in range(3)]
        )
        D[pl.ds(4 * g, 4)] = acc.reshape(4, 128, 256)

    loads[3].wait()

    def tap(a, b):
        return k2[(3 * a + b) * 256 : (3 * a + b) * 256 + 256, :]

    @pl.loop(0, 2)
    def _(g):
        for rp in range(2):
            for cp in range(2):
                terms = []
                for a, d in ((1, 0),) if rp == 0 else ((2, 0), (0, 1)):
                    for b, ref in ((1, C),) if cp == 0 else ((2, C), (0, Cs)):
                        terms.append(dot_nt(ref[pl.ds(4 * g + d, 4)].reshape(256, 512), tap(a, b)))
                acc = total_of(terms).reshape(4, 64, 256)
                for u in range(4):
                    B[2 * (4 * g + u) + rp, 64 * cp : 64 * cp + 64] = acc[u]

    def sides_of(cols_to):
        for side, ref, none in ((0, left, col == 0), (1, right, col == COLS - 1)):
            above = jnp.where((row == 0) | none, 0.0, cols_to[side, 0].astype(f32)[15:16])
            mid = jnp.where(none, 0.0, cols_to[side, 1].astype(f32))
            below = jnp.where((row == ROWS - 1) | none, 0.0, cols_to[side, 2].astype(f32)[0:1])
            ref[0:1] = above
            ref[1:17] = mid
            ref[17:18] = below

    for copy in halo:
        copy.wait_recv()
    sides_of(hcol)
    spread(16, jnp.where(row == 0, 0.0, hrow[0].astype(f32)))
    spread(17, jnp.where(row == ROWS - 1, 0.0, hrow[1].astype(f32)))
    for slot, r in ((16, 0), (17, 17)):
        shifted(X, r, columns_of(slot, 0), columns_of(slot, 1), left[r : r + 1], right[r : r + 1], True)
    top_at = lax.broadcasted_iota(jnp.int32, (16, 256), 0) == 0
    low_at = lax.broadcasted_iota(jnp.int32, (16, 256), 0) == 15
    for r in range(1, 17):
        X[r, 0:16, 0:256] = jnp.where(top_at, left[r : r + 1], X[r, 0:16, 0:256].astype(f32)).astype(bf16)
        X[r, 112:128, 512:768] = jnp.where(low_at, right[r : r + 1], X[r, 112:128, 512:768].astype(f32)).astype(bf16)
    D[0] += dot(X[0], k1[0:768, :])
    D[15] += dot(X[17], k1[1536:2304, :])
    for side, ref, b in ((0, left, 0), (1, right, 2)):
        ref[0:1] = jnp.zeros((1, 256), f32)
        ref[17:18] = jnp.zeros((1, 256), f32)
        fixes[side] = total_of(
            [dot(ref[a : a + 16].astype(bf16), k1[(3 * a + b) * 256 : (3 * a + b) * 256 + 256, :]) for a in range(3)]
        )
        at = 127 * side
        for p in range(16):
            D[p, at : at + 1] += fixes[side, p : p + 1]

    for copy in cot_halo:
        copy.wait_recv()
    no_right, no_below = col == COLS - 1, row == ROWS - 1
    beside = jnp.where(no_right, 0.0, ccol[0].astype(f32))
    corner = jnp.where(no_right | no_below, 0.0, ccol[1].astype(f32)[0:1])
    under = jnp.where(no_below, 0.0, crow[...].astype(f32))
    C[8] = under.astype(bf16)
    Cs[8] = jnp.where(end_at, corner, pltpu.roll(under, 63, 0)).astype(bf16)
    foot_at = lax.broadcasted_iota(jnp.int32, (16, 512), 0) == 15
    for i in range(8):
        Cs[i, 48:64] = jnp.where(foot_at, beside[i : i + 1], Cs[i, 48:64].astype(f32)).astype(bf16)
    @pl.loop(0, 8)
    def _(i):
        for rp in range(2):
            pre = D[2 * i + rp]
            s = jax.nn.sigmoid(pre)
            act = (pre * s).astype(bf16)
            for c in range(2):
                A[rp, c, i] = act[64 * c : 64 * c + 64]
            D[2 * i + rp] = s * (1.0 + pre * (1.0 - s))

    def axis_of(name):
        return (y, at_y, NY) if name == "y" else (x, at_x, NX)

    def places(job):
        j, base, rows, order = job
        place = JOBS.index(job)
        first = JOBS[place - 1][2] if place % 2 else 0
        o1, o2 = first // 4, first // 16
        return j, base, rows // 4, rows // 16, o1, o2, axis_of(order[0]), axis_of(order[1])

    def spans(job):
        j, base, n1, n2, o1, o2, (i1, _, _), (i2, _, _) = places(job)
        return base + n1 * i1, base + n1 * i1 + n2 * i2

    def al(v):
        return pl.multiple_of(v, 16)

    def stage1(n):
        j, base, n1, n2, o1, o2, (i1, to, _), _ = places(JOBS[n])
        return [
            send(
                S.at[j, pl.ds(al(base + n1 * ((i1 + k) % 4)), n1)], P1.at[n // 2, k - 1, pl.ds(o1, n1)],
                a1_s.at[n, k - 1], a1_r.at[n, k - 1], to(k),
            )
            for k in NEAR
        ]

    def stage2(n, arrived):
        j, base, n1, n2, o1, o2, (i1, _, _), (i2, to, _) = places(JOBS[n])
        for copy in arrived:
            copy.wait_recv()
        own = S[j, pl.ds(al(base + n1 * i1), n1)].astype(f32)
        Q1[n // 2, o1 : o1 + n1] = total_of([own] + [P1[n // 2, k, o1 : o1 + n1].astype(f32) for k in range(3)]).astype(bf16)
        return [
            send(
                Q1.at[n // 2, pl.ds(al(o1 + n2 * ((i2 + k) % 4)), n2)], P2.at[n // 2, k - 1, pl.ds(o2, n2)],
                a2_s.at[n, k - 1], a2_r.at[n, k - 1], to(k),
            )
            for k in NEAR
        ]

    def units_of(g):
        return JOBS[2 * g][2] // 256, JOBS[2 * g][2] // 256 + JOBS[2 * g + 1][2] // 256

    def stage_z(g, arrived):
        for copy in arrived:
            copy.wait_recv()
        for n in (2 * g, 2 * g + 1):
            _, base, n1, n2, o1, o2, _, (i2, _, _) = places(JOBS[n])
            own = Q1[g, pl.ds(al(o1 + n2 * i2), n2)].astype(f32)
            summed = total_of([own] + [P2[g, k, o2 : o2 + n2].astype(f32) for k in range(3)]).astype(bf16)
            for u in range(n2 // 16):
                unit = o2 // 16 + u
                block = summed[16 * u : 16 * u + 16]
                if unit < NZ:
                    Zs[g, unit, 0:16] = block
                else:
                    for k in range(NZ):
                        Zs[g, k, 16:32] = block
        for unit in range(units_of(g)[1], NZ):
            Zs[g, unit, 0:16] = jnp.zeros((16, 128), bf16)
        size = 32 if units_of(g)[1] > NZ else 16
        Zr[g, z, 0:size] = Zs[g, z, 0:size]
        return [
            send(
                Zs.at[g, (z + k) % NZ, pl.ds(0, size)], Zr.at[g, z, pl.ds(0, size)],
                az_s.at[g, k - 1], az_r.at[g, k - 1], at_z(k),
            )
            for k in ALONG_Z
        ]

    def gather_z(g, arrived):
        for copy in arrived:
            copy.wait_recv()
        first, units = units_of(g)
        size = 32 if units > NZ else 16
        summed = total_of([Zr[g, k, 0:size].astype(f32) for k in range(NZ)]).astype(bf16)
        j0, j1 = JOBS[2 * g][0], JOBS[2 * g + 1][0]
        at0, at1 = spans(JOBS[2 * g])[1], spans(JOBS[2 * g + 1])[1]
        second, unused = (z + 8 - first) // 8, (z + 8 - units) // 8 if units < NZ else 0
        mine = (1 - second) * (at0 + 16 * z) + (second - unused) * (at1 + 16 * (z - first)) + unused * (2304 + 128 * (g % 2) + 16 * z)
        j = j0 + second * (j1 - j0)
        G[j, core, pl.ds(al(mine), 16)] = summed[0:16]
        if units > NZ:
            G[j1, core, pl.ds(al(at1 + 16 * (NZ - first)), 16)] = summed[16:32]
        here = G.at[j, core, pl.ds(al(mine), 16)]
        return [send(here, here, gz_s.at[g, k - 1], gz_r.at[g, k - 1], at_z(k)) for k in ALONG_Z]

    def gather2(n, arrived):
        j, base, n1, n2, o1, o2, _, (i2, to, _) = places(JOBS[n])
        for copy in arrived:
            copy.wait_recv()
        here = G.at[j, core, pl.ds(al(spans(JOBS[n])[1]), n2)]
        return [send(here, here, g2_s.at[n, k - 1], g2_r.at[n, k - 1], to(k)) for k in NEAR]

    def to_sibling(n, k):
        j, base, n1, n2, o1, o2, (i1, _, _), _ = places(JOBS[n])
        here = G.at[j, core, pl.ds(al(base + n1 * ((i1 - k + 4) % 4)), n1)]
        return send(here, here, gc_s.at[n, k], gc_r.at[n, k], sibling)

    def gather1(n, arrived):
        j, base, n1, n2, o1, o2, (i1, to, _), _ = places(JOBS[n])
        for copy in arrived:
            copy.wait_recv()
        here = G.at[j, core, pl.ds(al(spans(JOBS[n])[0]), n1)]
        sent = [send(here, here, g1_s.at[n, k - 1], g1_r.at[n, k - 1], to(k)) for k in NEAR]
        return sent, [to_sibling(n, 0)]

    def forward(n, arrived):
        sent, across = arrived
        for i, k in enumerate(NEAR):
            sent[i].wait_recv()
            across.append(to_sibling(n, k))
        return across

    def two_taps(first_tap, last_tap, n):
        for m in range(first_tap, last_tap):
            a, b = m // 3, m % 3
            first = 1 if a == 0 else 0
            lhs = A[(a + 1) % 2, (b + 1) % 2].reshape(512, 256)
            rhs = (Cs if b == 0 else C)[first : first + 8].reshape(512, 512)
            out = dot_tn(lhs, rhs).astype(bf16)
            for h in range(2):
                T2[h, 256 * m : 256 * m + 256, :] = out[:, 256 * h : 256 * h + 256]
        span = pl.ds(256 * first_tap, 256 * (last_tap - first_tap))
        return send(T2.at[other, span], R2.at[span], c2_s.at[n], c2_r.at[n], sibling)

    def both_two(copies, first_tap, last_tap):
        for copy in copies:
            copy.wait_recv()

        @pl.loop(first_tap, last_tap)
        def _(g):
            span = pl.ds(pl.multiple_of(256 * g, 256), 256)
            both = T2[core, span].astype(f32) + R2[span].astype(f32)
            S[0, span] = both[:, :128].astype(bf16)
            S[1, span] = both[:, 128:].astype(bf16)

    def one_taps(first_tap, last_tap, n):
        for m in range(first_tap, last_tap):
            a, b = m // 3, m % 3
            lhs = X[a : a + 16, :, 256 * b : 256 * b + 256].reshape(2048, 256)
            out = dot_tn(lhs, V[1:17, :, 256:512].reshape(2048, 256)).astype(bf16)
            for h in range(2):
                T1[h, 256 * m : 256 * m + 256, :] = out[:, 128 * h : 128 * h + 128]
        span = pl.ds(256 * first_tap, 256 * (last_tap - first_tap))
        return send(T1.at[other, span], R1.at[span], c1_s.at[n], c1_r.at[n], sibling)

    def both_one(copies, first_tap, last_tap):
        for copy in copies:
            copy.wait_recv()

        @pl.loop(first_tap, last_tap)
        def _(g):
            span = pl.ds(pl.multiple_of(256 * g, 256), 256)
            S[2, span] = (T1[core, span].astype(f32) + R1[span].astype(f32)).astype(bf16)

    core_two = [two_taps(0, 3, 0), two_taps(3, 5, 1), two_taps(5, 7, 2), two_taps(7, 9, 3)]
    B[15, 0:64] += dot_nt(C[8], tap(0, 1))
    B[15, 64:128] += dot_nt(C[8], tap(0, 2)) + dot_nt(Cs[8], tap(0, 0))
    for a in range(3):
        fixes[a] = dot_nt(beside.astype(bf16), tap(a, 0))
    for i in range(8):
        B[2 * i, 127:128] += fixes[1, i : i + 1]
        below = fixes[2, i : i + 1]
        B[2 * i + 1, 127:128] += below + fixes[0, i + 1 : i + 2] if i < 7 else below

    @pl.loop(0, 16)
    def _(p):
        V[p + 1, :, 256:512] = (B[p] * D[p]).astype(bf16)

    for p in range(16):
        edge32[0, p : p + 1] = V[p + 1, 0:16, 256:512].astype(f32)[0:1]
        edge32[1, p : p + 1] = V[p + 1, 112:128, 256:512].astype(f32)[15:16]
    pedges[...] = edge32[...].astype(bf16)
    plast[0] = V[1, :, 256:512]
    plast[1] = V[16, :, 256:512]
    pg_halo = send_halos(plast.at[0], plast.at[1], pedges, prow, pcol, pg_s, pg_r)

    both_two(core_two[:2], 0, 5)
    g0 = [stage1(0), stage1(1)]
    core_one = [one_taps(0, 2, 0)]
    both_two(core_two[2:], 5, 9)
    g1 = [stage1(2), stage1(3)]
    core_one += [one_taps(2, 5, 1), one_taps(5, 7, 2)]
    both_one(core_one[:2], 0, 5)
    g2 = [stage1(4), stage1(5)]
    core_one += [one_taps(7, 9, 3)]
    both_one(core_one[2:], 5, 9)
    g3 = [stage1(6), stage1(7)]

    for copy in pg_halo:
        copy.wait_recv()
    sides_of(pcol)

    @pl.loop(0, 16)
    def _(p):
        shifted(
            V, p + 1, V[p + 1, 0:64, 256:512].astype(f32), V[p + 1, 64:128, 256:512].astype(f32),
            left[pl.ds(p + 1, 1)], right[pl.ds(p + 1, 1)], False,
        )

    for place, r, none in ((0, 0, row == 0), (1, 17, row == ROWS - 1)):
        values = jnp.where(none, 0.0, prow[place].astype(f32))
        shifted(V, r, values[0:64], values[64:128], left[r : r + 1], right[r : r + 1], True)

    def image_rows(g):
        terms = []
        for a in range(3):
            for b in range(3):
                m = 3 * (2 - a) + (2 - b)
                lhs = V[pl.ds(4 * g + a, 4), :, 256 * b : 256 * b + 256].reshape(512, 256)
                terms.append(dot_nt(lhs, k1[256 * m : 256 * m + 256, :]))
        acc = total_of(terms).reshape(4, 128, 256)
        for u in range(4):
            p = 4 * g + u
            for h in range(2):
                F[p, h, pl.ds(0, 64, stride=2), :] = acc[u, 0:64, 128 * h : 128 * h + 128]
                F[p, h, pl.ds(1, 64, stride=2), :] = acc[u, 64:128, 128 * h : 128 * h + 128]
            image_grad[p] = jnp.concatenate([F[p, 0], F[p, 1]], axis=1).astype(bf16)

    pl.loop(0, 1)(image_rows)

    def pair(step, g, arrived):
        return [step(2 * g, arrived[0]), step(2 * g + 1, arrived[1])]

    def both(arrived):
        return arrived[0] + arrived[1]

    def arrive(across):
        for copy in both(across):
            copy.wait_recv()

    g0 = pair(stage2, 0, g0)
    pl.loop(1, 3)(image_rows)
    g1 = pair(stage2, 1, g1)
    g0 = stage_z(0, both(g0))
    g2 = pair(stage2, 2, g2)
    g3 = pair(stage2, 3, g3)
    g1 = stage_z(1, both(g1))
    pl.loop(3, 4)(image_rows)
    g2 = stage_z(2, both(g2))
    g3 = stage_z(3, both(g3))
    g0 = gather_z(0, g0)
    g1 = gather_z(1, g1)
    g2 = gather_z(2, g2)
    g3 = gather_z(3, g3)
    g0 = pair(gather2, 0, [g0, []])
    g1 = pair(gather2, 1, [g1, []])
    g2 = pair(gather2, 2, [g2, []])
    g3 = pair(gather2, 3, [g3, []])
    g0 = pair(gather1, 0, g0)
    g1 = pair(gather1, 1, g1)
    g2 = pair(gather1, 2, g2)
    g3 = pair(gather1, 3, g3)
    g0 = pair(forward, 0, g0)
    g1 = pair(forward, 1, g1)

    def squares_of(buffers):
        def add(g, acc):
            span = pl.ds(pl.multiple_of(256 * g, 256), 256)
            for j in buffers:
                for c in range(2):
                    v = G[j, c, span].astype(f32).reshape(32, 8, 128)
                    acc = acc + jnp.sum(v * v, axis=0)
            return acc

        return lax.fori_loop(0, 9, add, jnp.zeros((8, 128), f32))

    g2 = pair(forward, 2, g2)
    arrive(g0)
    arrive(g1)
    sum_two = jnp.sum(squares_of((0, 1)))
    g3 = pair(forward, 3, g3)
    scale_two = lax.rsqrt(sum_two / (9.0 * 256 * 512) + 1e-06)

    @pl.loop(0, 9)
    def _(g):
        span = pl.ds(pl.multiple_of(256 * g, 256), 256)
        for c in range(2):
            for j in range(2):
                two[span, 256 * c + 128 * j : 256 * c + 128 * j + 128] = (G[j, c, span].astype(f32) * scale_two).astype(bf16)

    arrive(g2)
    arrive(g3)
    squares[...] = squares_of((2,))

    for copy in pending:
        copy.wait_send()


def written(rows, two_v, G, squares, image_grad, two, one, one_v, sem):
    copies = [pltpu.make_async_copy(rows, image_grad, sem.at[0]), pltpu.make_async_copy(two_v, two, sem.at[1])]
    for copy in copies:
        copy.start()
    scale = lax.rsqrt(jnp.sum(squares[...]) / (9.0 * 256 * 256) + 1e-06)
    for a in range(3):
        span = pl.ds(768 * a, 768)
        for c in range(2):
            one_v[span, 128 * c : 128 * c + 128] = (G[2, c, span].astype(f32) * scale).astype(bf16)
        copies.append(pltpu.make_async_copy(one_v.at[span], one.at[span], sem.at[2 + a]))
        copies[-1].start()
    for copy in copies:
        copy.wait()


def on_device(image, kernel_one, kernel_two, cotangent):
    vmem = pl.BlockSpec(memory_space=pltpu.VMEM)
    hbm = pl.BlockSpec(memory_space=pl.ANY)
    dma = pltpu.SemaphoreType.DMA
    pairs = [(8,), (3,), (8,), (4,), (4,), (8, 3), (8, 3), (4, 7), (4, 7), (8, 3), (8, 3), (8, 4)]
    scratch = [
        ((16, 128, 256), bf16), ((2304, 256), bf16), ((2304, 512), bf16), ((8, 64, 512), bf16),
        ((18, 2, 128, 128), f32), ((18, 128, 768), bf16), ((18, 128, 768), bf16),
        ((2, 2, 8, 64, 256), bf16), ((16, 128, 256), f32), ((16, 128, 256), f32), ((9, 64, 512), bf16), ((9, 64, 512), bf16),
        ((2, 16, 256), f32), ((2, 16, 256), bf16), ((2, 128, 256), bf16), ((2, 3, 16, 256), bf16),
        ((16, 512), bf16), ((64, 512), bf16), ((2, 16, 512), bf16),
        ((2, 16, 256), bf16), ((2, 128, 256), bf16), ((2, 128, 256), bf16), ((2, 3, 16, 256), bf16),
        ((24, 256), f32), ((24, 256), f32), ((3, 16, 256), f32),
        ((2, 2304, 256), bf16), ((2304, 256), bf16), ((2, 2304, 128), bf16), ((2304, 128), bf16),
        ((3, 2304, 128), bf16), ((4, 3, 576, 128), bf16), ((4, 576, 128), bf16), ((4, 3, 144, 128), bf16),
        ((4, 8, 32, 128), bf16), ((4, 8, 32, 128), bf16),
    ]
    kept = [pltpu.VMEM(s, d) for s, d in (((16, 128, 256), bf16), ((2304, 512), bf16), ((3, 2, 2560, 128), bf16), ((8, 128), f32))]
    kept_arrays = pl.pallas_call(
        kernel,
        out_shape=kept,
        in_specs=[hbm] * 4,
        out_specs=[vmem] * 4,
        scratch_shapes=[pltpu.VMEM(shape, kind) for shape, kind in scratch] + [dma((4,))] + [dma(s) for s in pairs for _ in range(2)],
        compiler_params=pltpu.CompilerParams(collective_id=0, has_side_effects=True, vmem_limit_bytes=50 << 20),
    )(image, kernel_one.reshape(2304, 256), kernel_two.reshape(2304, 512), cotangent)
    image_grad, two, one = pl.pallas_call(
        written,
        out_shape=(
            jax.ShapeDtypeStruct((16, 128, 256), bf16),
            jax.ShapeDtypeStruct((2304, 512), bf16),
            jax.ShapeDtypeStruct((2304, 256), bf16),
        ),
        in_specs=[vmem] * 4,
        out_specs=[hbm] * 3,
        scratch_shapes=[pltpu.VMEM((2304, 256), bf16), dma((5,))],
        compiler_params=pltpu.CompilerParams(vmem_limit_bytes=16 << 20),
    )(*kept_arrays)
    return image_grad, one.reshape(kernel_one.shape), two.reshape(kernel_two.shape)


def solution(mesh):
    placed = (P("row", "col", None), P(), P(), P("row", "col", None))
    return jax.shard_map(
        on_device, mesh=mesh, in_specs=placed, out_specs=(P("row", "col", None), P(), P()), check_vma=False
    )
```

```python
import functools

import jax
import jax.numpy as jnp
from jax import lax
from jax.experimental import pallas as pl
from jax.experimental.pallas import tpu as pltpu
from jax.sharding import PartitionSpec as P

MESH = pl.DeviceIdType.MESH
bf16, f32 = jnp.bfloat16, jnp.float32
ROWS, COLS = 32, 8
NX, NY, NZ = 4, 4, 8
NEAR, ALONG_Z = (2, 1, 3), (4, 3, 5, 2, 6, 1, 7)
JOBS = (
    (0, 0, 1280, "yx"), (1, 0, 1024, "xy"),
    (0, 1280, 1024, "yx"), (1, 1024, 1280, "xy"),
    (2, 0, 768, "yx"), (2, 768, 512, "xy"),
    (2, 1280, 512, "yx"), (2, 1792, 512, "xy"),
)


def dot(a, b):
    return jnp.dot(a, b, preferred_element_type=f32)


def dot_nt(a, b):
    return lax.dot_general(a, b, (((1,), (1,)), ((), ())), preferred_element_type=f32)


def dot_tn(a, b):
    return lax.dot_general(a, b, (((0,), (0,)), ((), ())), preferred_element_type=f32)


def total_of(terms):
    return functools.reduce(lambda u, v: u + v, terms)


def kernel(
    image_hbm, k1_hbm, k2_hbm, cot_hbm,
    image_grad, two, G, squares,
    image, k1, k2, cot, F, X, V, A, D, B, C, Cs,
    edge32, edges, hrow, hcol, cedge, crow, ccol, pedges, plast, prow, pcol, left, right, fixes,
    T2, R2, T1, R1, S, P1, Q1, P2, Zs, Zr,
    load_sem,
    img_s, img_r, cot_s, cot_r, pg_s, pg_r, c2_s, c2_r, c1_s, c1_r,
    a1_s, a1_r, a2_s, a2_r, az_s, az_r, gz_s, gz_r, g2_s, g2_r, g1_s, g1_r, gc_s, gc_r,
):
    row, col = lax.axis_index("row"), lax.axis_index("col")
    z, x, y, core = row // NX, row % NX, col // 2, col % 2
    other = 1 - core

    def at_row(d):
        return (row + d + ROWS) % ROWS

    def at_col(d):
        return (col + d + COLS) % COLS

    def at_x(k):
        return (z * NX + (x + k) % NX, col)

    def at_y(k):
        return (row, ((y + k) % NY) * 2 + core)

    def at_z(k):
        return (((z + k) % NZ) * NX + x, col)

    sibling = (row, y * 2 + other)
    around = [(at_row(u), at_col(v)) for u in (-1, 0, 1) for v in (-1, 0, 1) if (u, v) != (0, 0)]
    pending = []

    def send(src, dst, send_sem, recv_sem, to):
        copy = pltpu.make_async_remote_copy(
            src_ref=src, dst_ref=dst, send_sem=send_sem, recv_sem=recv_sem, device_id=to, device_id_type=MESH
        )
        copy.start()
        pending.append(copy)
        return copy

    loads = []
    for n, (src, dst) in enumerate(((image_hbm, image), (cot_hbm, cot), (k1_hbm, k1), (k2_hbm, k2))):
        copy = pltpu.make_async_copy(src, dst, load_sem.at[n])
        copy.start()
        loads.append(copy)

    barrier = pltpu.get_barrier_semaphore()
    greeted = around + [sibling] + [at_y(k) for k in (1, 2, 3)] + [at_x(k) for k in (1, 2, 3)] + [at_z(k) for k in range(1, NZ)]
    for to in greeted:
        pl.semaphore_signal(barrier, inc=1, device_id=to, device_id_type=MESH)

    def spread(slot, values):
        v = values.astype(f32)
        F[slot, 0] = v[:, :128]
        F[slot, 1] = v[:, 128:]

    loads[0].wait()

    @pl.loop(0, 16)
    def _(p):
        spread(p, image[p])

    for p in range(16):
        for h in range(2):
            edge32[0, p : p + 1, 128 * h : 128 * h + 128] = F[p, h, 0:1, :]
            edge32[1, p : p + 1, 128 * h : 128 * h + 128] = F[p, h, 127:128, :]
    edges[...] = edge32[...].astype(bf16)

    first_at = lax.broadcasted_iota(jnp.int32, (64, 256), 0) == 0
    last_at = lax.broadcasted_iota(jnp.int32, (64, 256), 0) == 63

    def shifted(ref, r, even, odd, before_first, after_last, centre):
        before = jnp.where(first_at, before_first, pltpu.roll(odd, 1, 0)).astype(bf16)
        after = jnp.where(last_at, after_last, pltpu.roll(even, 63, 0)).astype(bf16)
        e, o = even.astype(bf16), odd.astype(bf16)
        ref[r, 0:64, 0:256] = before
        ref[r, 64:128, 0:256] = e
        if centre:
            ref[r, 0:64, 256:512] = e
            ref[r, 64:128, 256:512] = o
        ref[r, 0:64, 512:768] = o
        ref[r, 64:128, 512:768] = after

    def columns_of(slot, odd):
        return jnp.concatenate([F[slot, h, pl.ds(odd, 64, stride=2), :] for h in (0, 1)], axis=1)

    @pl.loop(0, 16)
    def _(p):
        shifted(X, p + 1, columns_of(p, 0), columns_of(p, 1), 0.0, 0.0, True)

    X[0] = jnp.zeros((128, 768), bf16)
    X[17] = jnp.zeros((128, 768), bf16)

    loads[1].wait()
    edge2 = [cot[i, 0:16, :].astype(f32)[0:1] for i in range(8)]
    cedge[...] = jnp.concatenate(edge2 + [jnp.zeros((8, 512), f32)], axis=0).astype(bf16)
    pl.semaphore_wait(barrier, len(greeted))

    def send_halos(first, last, ends, rows_to, cols_to, send_sem, recv_sem):
        sent = [
            send(first, rows_to.at[1], send_sem.at[0], recv_sem.at[0], (at_row(-1), col)),
            send(last, rows_to.at[0], send_sem.at[1], recv_sem.at[1], (at_row(1), col)),
        ]
        n = 2
        for side, v in ((1, -1), (0, 1)):
            for place, u in ((0, 1), (1, 0), (2, -1)):
                to = (at_row(u) if u else row, at_col(v))
                sent.append(send(ends.at[1 - side], cols_to.at[side, place], send_sem.at[n], recv_sem.at[n], to))
                n += 1
        return sent

    halo = send_halos(image.at[0], image.at[15], edges, hrow, hcol, img_s, img_r)
    cot_halo = [
        send(cot.at[0], crow, cot_s.at[0], cot_r.at[0], (at_row(-1), col)),
        send(cedge, ccol.at[0], cot_s.at[1], cot_r.at[1], (row, at_col(-1))),
        send(cedge, ccol.at[1], cot_s.at[2], cot_r.at[2], (at_row(-1), at_col(-1))),
    ]

    end_at = lax.broadcasted_iota(jnp.int32, (64, 512), 0) == 63
    for i in range(8):
        C[i] = cot[i]
        Cs[i] = jnp.where(end_at, 0.0, pltpu.roll(cot[i].astype(f32), 63, 0)).astype(bf16)
    C[8] = jnp.zeros((64, 512), bf16)
    Cs[8] = jnp.zeros((64, 512), bf16)

    loads[2].wait()

    @pl.loop(0, 4)
    def _(g):
        acc = total_of(
            [dot(X[pl.ds(4 * g + a, 4)].reshape(512, 768), k1[768 * a : 768 * a + 768, :]) for a in range(3)]
        )
        D[pl.ds(4 * g, 4)] = acc.reshape(4, 128, 256)

    loads[3].wait()

    def tap(a, b):
        return k2[(3 * a + b) * 256 : (3 * a + b) * 256 + 256, :]

    @pl.loop(0, 2)
    def _(g):
        for rp in range(2):
            for cp in range(2):
                terms = []
                for a, d in ((1, 0),) if rp == 0 else ((2, 0), (0, 1)):
                    for b, ref in ((1, C),) if cp == 0 else ((2, C), (0, Cs)):
                        terms.append(dot_nt(ref[pl.ds(4 * g + d, 4)].reshape(256, 512), tap(a, b)))
                acc = total_of(terms).reshape(4, 64, 256)
                for u in range(4):
                    B[2 * (4 * g + u) + rp, 64 * cp : 64 * cp + 64] = acc[u]

    def sides_of(cols_to):
        for side, ref, none in ((0, left, col == 0), (1, right, col == COLS - 1)):
            above = jnp.where((row == 0) | none, 0.0, cols_to[side, 0].astype(f32)[15:16])
            mid = jnp.where(none, 0.0, cols_to[side, 1].astype(f32))
            below = jnp.where((row == ROWS - 1) | none, 0.0, cols_to[side, 2].astype(f32)[0:1])
            ref[0:1] = above
            ref[1:17] = mid
            ref[17:18] = below

    for copy in halo:
        copy.wait_recv()
    sides_of(hcol)
    spread(16, jnp.where(row == 0, 0.0, hrow[0].astype(f32)))
    spread(17, jnp.where(row == ROWS - 1, 0.0, hrow[1].astype(f32)))
    for slot, r in ((16, 0), (17, 17)):
        shifted(X, r, columns_of(slot, 0), columns_of(slot, 1), left[r : r + 1], right[r : r + 1], True)
    top_at = lax.broadcasted_iota(jnp.int32, (16, 256), 0) == 0
    low_at = lax.broadcasted_iota(jnp.int32, (16, 256), 0) == 15
    for r in range(1, 17):
        X[r, 0:16, 0:256] = jnp.where(top_at, left[r : r + 1], X[r, 0:16, 0:256].astype(f32)).astype(bf16)
        X[r, 112:128, 512:768] = jnp.where(low_at, right[r : r + 1], X[r, 112:128, 512:768].astype(f32)).astype(bf16)
    D[0] += dot(X[0], k1[0:768, :])
    D[15] += dot(X[17], k1[1536:2304, :])
    for side, ref, b in ((0, left, 0), (1, right, 2)):
        ref[0:1] = jnp.zeros((1, 256), f32)
        ref[17:18] = jnp.zeros((1, 256), f32)
        fixes[side] = total_of(
            [dot(ref[a : a + 16].astype(bf16), k1[(3 * a + b) * 256 : (3 * a + b) * 256 + 256, :]) for a in range(3)]
        )
        at = 127 * side
        for p in range(16):
            D[p, at : at + 1] += fixes[side, p : p + 1]

    for copy in cot_halo:
        copy.wait_recv()
    no_right, no_below = col == COLS - 1, row == ROWS - 1
    beside = jnp.where(no_right, 0.0, ccol[0].astype(f32))
    corner = jnp.where(no_right | no_below, 0.0, ccol[1].astype(f32)[0:1])
    under = jnp.where(no_below, 0.0, crow[...].astype(f32))
    C[8] = under.astype(bf16)
    Cs[8] = jnp.where(end_at, corner, pltpu.roll(under, 63, 0)).astype(bf16)
    foot_at = lax.broadcasted_iota(jnp.int32, (16, 512), 0) == 15
    for i in range(8):
        Cs[i, 48:64] = jnp.where(foot_at, beside[i : i + 1], Cs[i, 48:64].astype(f32)).astype(bf16)
    @pl.loop(0, 8)
    def _(i):
        for rp in range(2):
            pre = D[2 * i + rp]
            s = jax.nn.sigmoid(pre)
            act = (pre * s).astype(bf16)
            for c in range(2):
                A[rp, c, i] = act[64 * c : 64 * c + 64]
            D[2 * i + rp] = s * (1.0 + pre * (1.0 - s))

    def axis_of(name):
        return (y, at_y, NY) if name == "y" else (x, at_x, NX)

    def places(job):
        j, base, rows, order = job
        place = JOBS.index(job)
        first = JOBS[place - 1][2] if place % 2 else 0
        o1, o2 = first // 4, first // 16
        return j, base, rows // 4, rows // 16, o1, o2, axis_of(order[0]), axis_of(order[1])

    def spans(job):
        j, base, n1, n2, o1, o2, (i1, _, _), (i2, _, _) = places(job)
        return base + n1 * i1, base + n1 * i1 + n2 * i2

    def al(v):
        return pl.multiple_of(v, 16)

    def stage1(n):
        j, base, n1, n2, o1, o2, (i1, to, _), _ = places(JOBS[n])
        return [
            send(
                S.at[j, pl.ds(al(base + n1 * ((i1 + k) % 4)), n1)], P1.at[n // 2, k - 1, pl.ds(o1, n1)],
                a1_s.at[n, k - 1], a1_r.at[n, k - 1], to(k),
            )
            for k in NEAR
        ]

    def stage2(n, arrived):
        j, base, n1, n2, o1, o2, (i1, _, _), (i2, to, _) = places(JOBS[n])
        for copy in arrived:
            copy.wait_recv()
        own = S[j, pl.ds(al(base + n1 * i1), n1)].astype(f32)
        Q1[n // 2, o1 : o1 + n1] = total_of([own] + [P1[n // 2, k, o1 : o1 + n1].astype(f32) for k in range(3)]).astype(bf16)
        return [
            send(
                Q1.at[n // 2, pl.ds(al(o1 + n2 * ((i2 + k) % 4)), n2)], P2.at[n // 2, k - 1, pl.ds(o2, n2)],
                a2_s.at[n, k - 1], a2_r.at[n, k - 1], to(k),
            )
            for k in NEAR
        ]

    def units_of(g):
        return JOBS[2 * g][2] // 256, JOBS[2 * g][2] // 256 + JOBS[2 * g + 1][2] // 256

    def stage_z(g, arrived):
        for copy in arrived:
            copy.wait_recv()
        for n in (2 * g, 2 * g + 1):
            _, base, n1, n2, o1, o2, _, (i2, _, _) = places(JOBS[n])
            own = Q1[g, pl.ds(al(o1 + n2 * i2), n2)].astype(f32)
            summed = total_of([own] + [P2[g, k, o2 : o2 + n2].astype(f32) for k in range(3)]).astype(bf16)
            for u in range(n2 // 16):
                unit = o2 // 16 + u
                block = summed[16 * u : 16 * u + 16]
                if unit < NZ:
                    Zs[g, unit, 0:16] = block
                else:
                    for k in range(NZ):
                        Zs[g, k, 16:32] = block
        for unit in range(units_of(g)[1], NZ):
            Zs[g, unit, 0:16] = jnp.zeros((16, 128), bf16)
        size = 32 if units_of(g)[1] > NZ else 16
        Zr[g, z, 0:size] = Zs[g, z, 0:size]
        return [
            send(
                Zs.at[g, (z + k) % NZ, pl.ds(0, size)], Zr.at[g, z, pl.ds(0, size)],
                az_s.at[g, k - 1], az_r.at[g, k - 1], at_z(k),
            )
            for k in ALONG_Z
        ]

    def gather_z(g, arrived):
        for copy in arrived:
            copy.wait_recv()
        first, units = units_of(g)
        size = 32 if units > NZ else 16
        summed = total_of([Zr[g, k, 0:size].astype(f32) for k in range(NZ)]).astype(bf16)
        j0, j1 = JOBS[2 * g][0], JOBS[2 * g + 1][0]
        at0, at1 = spans(JOBS[2 * g])[1], spans(JOBS[2 * g + 1])[1]
        second, unused = (z + 8 - first) // 8, (z + 8 - units) // 8 if units < NZ else 0
        mine = (1 - second) * (at0 + 16 * z) + (second - unused) * (at1 + 16 * (z - first)) + unused * (2304 + 128 * (g % 2) + 16 * z)
        j = j0 + second * (j1 - j0)
        G[j, core, pl.ds(al(mine), 16)] = summed[0:16]
        if units > NZ:
            G[j1, core, pl.ds(al(at1 + 16 * (NZ - first)), 16)] = summed[16:32]
        here = G.at[j, core, pl.ds(al(mine), 16)]
        return [send(here, here, gz_s.at[g, k - 1], gz_r.at[g, k - 1], at_z(k)) for k in ALONG_Z]

    def gather2(n, arrived):
        j, base, n1, n2, o1, o2, _, (i2, to, _) = places(JOBS[n])
        for copy in arrived:
            copy.wait_recv()
        here = G.at[j, core, pl.ds(al(spans(JOBS[n])[1]), n2)]
        return [send(here, here, g2_s.at[n, k - 1], g2_r.at[n, k - 1], to(k)) for k in NEAR]

    def to_sibling(n, k):
        j, base, n1, n2, o1, o2, (i1, _, _), _ = places(JOBS[n])
        here = G.at[j, core, pl.ds(al(base + n1 * ((i1 - k + 4) % 4)), n1)]
        return send(here, here, gc_s.at[n, k], gc_r.at[n, k], sibling)

    def gather1(n, arrived):
        j, base, n1, n2, o1, o2, (i1, to, _), _ = places(JOBS[n])
        for copy in arrived:
            copy.wait_recv()
        here = G.at[j, core, pl.ds(al(spans(JOBS[n])[0]), n1)]
        sent = [send(here, here, g1_s.at[n, k - 1], g1_r.at[n, k - 1], to(k)) for k in NEAR]
        return sent, [to_sibling(n, 0)]

    def forward(n, arrived):
        sent, across = arrived
        for i, k in enumerate(NEAR):
            sent[i].wait_recv()
            across.append(to_sibling(n, k))
        return across

    def two_taps(first_tap, last_tap, n):
        for m in range(first_tap, last_tap):
            a, b = m // 3, m % 3
            first = 1 if a == 0 else 0
            lhs = A[(a + 1) % 2, (b + 1) % 2].reshape(512, 256)
            rhs = (Cs if b == 0 else C)[first : first + 8].reshape(512, 512)
            out = dot_tn(lhs, rhs).astype(bf16)
            for h in range(2):
                T2[h, 256 * m : 256 * m + 256, :] = out[:, 256 * h : 256 * h + 256]
        span = pl.ds(256 * first_tap, 256 * (last_tap - first_tap))
        return send(T2.at[other, span], R2.at[span], c2_s.at[n], c2_r.at[n], sibling)

    def both_two(copies, first_tap, last_tap):
        for copy in copies:
            copy.wait_recv()

        @pl.loop(first_tap, last_tap)
        def _(g):
            span = pl.ds(pl.multiple_of(256 * g, 256), 256)
            both = T2[core, span].astype(f32) + R2[span].astype(f32)
            S[0, span] = both[:, :128].astype(bf16)
            S[1, span] = both[:, 128:].astype(bf16)

    def one_taps(first_tap, last_tap, n):
        for m in range(first_tap, last_tap):
            a, b = m // 3, m % 3
            lhs = X[a : a + 16, :, 256 * b : 256 * b + 256].reshape(2048, 256)
            out = dot_tn(lhs, V[1:17, :, 256:512].reshape(2048, 256)).astype(bf16)
            for h in range(2):
                T1[h, 256 * m : 256 * m + 256, :] = out[:, 128 * h : 128 * h + 128]
        span = pl.ds(256 * first_tap, 256 * (last_tap - first_tap))
        return send(T1.at[other, span], R1.at[span], c1_s.at[n], c1_r.at[n], sibling)

    def both_one(copies, first_tap, last_tap):
        for copy in copies:
            copy.wait_recv()

        @pl.loop(first_tap, last_tap)
        def _(g):
            span = pl.ds(pl.multiple_of(256 * g, 256), 256)
            S[2, span] = (T1[core, span].astype(f32) + R1[span].astype(f32)).astype(bf16)

    core_two = [two_taps(0, 3, 0), two_taps(3, 5, 1), two_taps(5, 7, 2), two_taps(7, 9, 3)]
    B[15, 0:64] += dot_nt(C[8], tap(0, 1))
    B[15, 64:128] += dot_nt(C[8], tap(0, 2)) + dot_nt(Cs[8], tap(0, 0))
    for a in range(3):
        fixes[a] = dot_nt(beside.astype(bf16), tap(a, 0))
    for i in range(8):
        B[2 * i, 127:128] += fixes[1, i : i + 1]
        below = fixes[2, i : i + 1]
        B[2 * i + 1, 127:128] += below + fixes[0, i + 1 : i + 2] if i < 7 else below

    @pl.loop(0, 16)
    def _(p):
        V[p + 1, :, 256:512] = (B[p] * D[p]).astype(bf16)

    for p in range(16):
        edge32[0, p : p + 1] = V[p + 1, 0:16, 256:512].astype(f32)[0:1]
        edge32[1, p : p + 1] = V[p + 1, 112:128, 256:512].astype(f32)[15:16]
    pedges[...] = edge32[...].astype(bf16)
    plast[0] = V[1, :, 256:512]
    plast[1] = V[16, :, 256:512]
    pg_halo = send_halos(plast.at[0], plast.at[1], pedges, prow, pcol, pg_s, pg_r)

    both_two(core_two[:2], 0, 5)
    g0 = [stage1(0), stage1(1)]
    core_one = [one_taps(0, 2, 0)]
    both_two(core_two[2:], 5, 9)
    g1 = [stage1(2), stage1(3)]
    core_one += [one_taps(2, 5, 1), one_taps(5, 7, 2)]
    both_one(core_one[:2], 0, 5)
    g2 = [stage1(4), stage1(5)]
    core_one += [one_taps(7, 9, 3)]
    both_one(core_one[2:], 5, 9)
    g3 = [stage1(6), stage1(7)]

    def image_rows(g):
        terms = []
        for a in range(3):
            for b in range(3):
                m = 3 * (2 - a) + (2 - b)
                lhs = V[pl.ds(4 * g + a, 4), :, 256 * b : 256 * b + 256].reshape(512, 256)
                terms.append(dot_nt(lhs, k1[256 * m : 256 * m + 256, :]))
        acc = total_of(terms).reshape(4, 128, 256)
        for u in range(4):
            p = 4 * g + u
            for h in range(2):
                F[p, h, pl.ds(0, 64, stride=2), :] = acc[u, 0:64, 128 * h : 128 * h + 128]
                F[p, h, pl.ds(1, 64, stride=2), :] = acc[u, 64:128, 128 * h : 128 * h + 128]
            image_grad[p] = jnp.concatenate([F[p, 0], F[p, 1]], axis=1).astype(bf16)


    def pair(step, g, arrived):
        return [step(2 * g, arrived[0]), step(2 * g + 1, arrived[1])]

    def both(arrived):
        return arrived[0] + arrived[1]

    def arrive(across):
        for copy in both(across):
            copy.wait_recv()

    g0 = pair(stage2, 0, g0)

    for copy in pg_halo:
        copy.wait_recv()
    sides_of(pcol)

    @pl.loop(0, 16)
    def _(p):
        shifted(
            V, p + 1, V[p + 1, 0:64, 256:512].astype(f32), V[p + 1, 64:128, 256:512].astype(f32),
            left[pl.ds(p + 1, 1)], right[pl.ds(p + 1, 1)], False,
        )

    for place, r, none in ((0, 0, row == 0), (1, 17, row == ROWS - 1)):
        values = jnp.where(none, 0.0, prow[place].astype(f32))
        shifted(V, r, values[0:64], values[64:128], left[r : r + 1], right[r : r + 1], True)

    pl.loop(0, 2)(image_rows)
    g1 = pair(stage2, 1, g1)
    g0 = stage_z(0, both(g0))
    g2 = pair(stage2, 2, g2)
    g3 = pair(stage2, 3, g3)
    g1 = stage_z(1, both(g1))
    pl.loop(2, 3)(image_rows)
    g2 = stage_z(2, both(g2))
    g3 = stage_z(3, both(g3))
    pl.loop(3, 4)(image_rows)
    g0 = gather_z(0, g0)
    g1 = gather_z(1, g1)
    g2 = gather_z(2, g2)
    g3 = gather_z(3, g3)
    g0 = pair(gather2, 0, [g0, []])
    g1 = pair(gather2, 1, [g1, []])
    g2 = pair(gather2, 2, [g2, []])
    g3 = pair(gather2, 3, [g3, []])
    g0 = pair(gather1, 0, g0)
    g1 = pair(gather1, 1, g1)
    g2 = pair(gather1, 2, g2)
    g3 = pair(gather1, 3, g3)
    g0 = pair(forward, 0, g0)
    g1 = pair(forward, 1, g1)

    def squares_of(buffers):
        def add(g, acc):
            span = pl.ds(pl.multiple_of(256 * g, 256), 256)
            for j in buffers:
                for c in range(2):
                    v = G[j, c, span].astype(f32).reshape(32, 8, 128)
                    acc = acc + jnp.sum(v * v, axis=0)
            return acc

        return lax.fori_loop(0, 9, add, jnp.zeros((8, 128), f32))

    g2 = pair(forward, 2, g2)
    arrive(g0)
    arrive(g1)
    sum_two = jnp.sum(squares_of((0, 1)))
    g3 = pair(forward, 3, g3)
    scale_two = lax.rsqrt(sum_two / (9.0 * 256 * 512) + 1e-06)

    @pl.loop(0, 9)
    def _(g):
        span = pl.ds(pl.multiple_of(256 * g, 256), 256)
        for c in range(2):
            for j in range(2):
                two[span, 256 * c + 128 * j : 256 * c + 128 * j + 128] = (G[j, c, span].astype(f32) * scale_two).astype(bf16)

    arrive(g2)
    arrive(g3)
    squares[...] = squares_of((2,))

    for copy in pending:
        copy.wait_send()


def written(rows, two_v, G, squares, image_grad, two, one, one_v, sem):
    copies = [pltpu.make_async_copy(rows, image_grad, sem.at[0]), pltpu.make_async_copy(two_v, two, sem.at[1])]
    for copy in copies:
        copy.start()
    scale = lax.rsqrt(jnp.sum(squares[...]) / (9.0 * 256 * 256) + 1e-06)
    for a in range(3):
        span = pl.ds(768 * a, 768)
        for c in range(2):
            one_v[span, 128 * c : 128 * c + 128] = (G[2, c, span].astype(f32) * scale).astype(bf16)
        copies.append(pltpu.make_async_copy(one_v.at[span], one.at[span], sem.at[2 + a]))
        copies[-1].start()
    for copy in copies:
        copy.wait()


def on_device(image, kernel_one, kernel_two, cotangent):
    vmem = pl.BlockSpec(memory_space=pltpu.VMEM)
    hbm = pl.BlockSpec(memory_space=pl.ANY)
    dma = pltpu.SemaphoreType.DMA
    pairs = [(8,), (3,), (8,), (4,), (4,), (8, 3), (8, 3), (4, 7), (4, 7), (8, 3), (8, 3), (8, 4)]
    scratch = [
        ((16, 128, 256), bf16), ((2304, 256), bf16), ((2304, 512), bf16), ((8, 64, 512), bf16),
        ((18, 2, 128, 128), f32), ((18, 128, 768), bf16), ((18, 128, 768), bf16),
        ((2, 2, 8, 64, 256), bf16), ((16, 128, 256), f32), ((16, 128, 256), f32), ((9, 64, 512), bf16), ((9, 64, 512), bf16),
        ((2, 16, 256), f32), ((2, 16, 256), bf16), ((2, 128, 256), bf16), ((2, 3, 16, 256), bf16),
        ((16, 512), bf16), ((64, 512), bf16), ((2, 16, 512), bf16),
        ((2, 16, 256), bf16), ((2, 128, 256), bf16), ((2, 128, 256), bf16), ((2, 3, 16, 256), bf16),
        ((24, 256), f32), ((24, 256), f32), ((3, 16, 256), f32),
        ((2, 2304, 256), bf16), ((2304, 256), bf16), ((2, 2304, 128), bf16), ((2304, 128), bf16),
        ((3, 2304, 128), bf16), ((4, 3, 576, 128), bf16), ((4, 576, 128), bf16), ((4, 3, 144, 128), bf16),
        ((4, 8, 32, 128), bf16), ((4, 8, 32, 128), bf16),
    ]
    kept = [pltpu.VMEM(s, d) for s, d in (((16, 128, 256), bf16), ((2304, 512), bf16), ((3, 2, 2560, 128), bf16), ((8, 128), f32))]
    kept_arrays = pl.pallas_call(
        kernel,
        out_shape=kept,
        in_specs=[hbm] * 4,
        out_specs=[vmem] * 4,
        scratch_shapes=[pltpu.VMEM(shape, kind) for shape, kind in scratch] + [dma((4,))] + [dma(s) for s in pairs for _ in range(2)],
        compiler_params=pltpu.CompilerParams(collective_id=0, has_side_effects=True, vmem_limit_bytes=50 << 20),
    )(image, kernel_one.reshape(2304, 256), kernel_two.reshape(2304, 512), cotangent)
    image_grad, two, one = pl.pallas_call(
        written,
        out_shape=(
            jax.ShapeDtypeStruct((16, 128, 256), bf16),
            jax.ShapeDtypeStruct((2304, 512), bf16),
            jax.ShapeDtypeStruct((2304, 256), bf16),
        ),
        in_specs=[vmem] * 4,
        out_specs=[hbm] * 3,
        scratch_shapes=[pltpu.VMEM((2304, 256), bf16), dma((5,))],
        compiler_params=pltpu.CompilerParams(vmem_limit_bytes=16 << 20),
    )(*kept_arrays)
    return image_grad, one.reshape(kernel_one.shape), two.reshape(kernel_two.shape)


def solution(mesh):
    placed = (P("row", "col", None), P(), P(), P("row", "col", None))
    return jax.shard_map(
        on_device, mesh=mesh, in_specs=placed, out_specs=(P("row", "col", None), P(), P()), check_vma=False
    )
```
